128 devices in a mesh: node: 8 (over y, core), fsdp: 16 (over z, x).
Axes of the slice: x: 4, y: 4, z: 4, core: 2. Of those that a mesh axis runs over, the one named last changes fastest.
Arguments:
- activations: bfloat16 [131072, 2560], P(('node', 'fsdp'))
- grad_out: bfloat16 [131072, 2560], P(('node', 'fsdp'))
Outputs:
- combined: float32 [2560, 2560], P('fsdp', 'node')
All inputs are finite; a program needn't handle non-finite values.
Results may differ from the reference program's by a relative error of at most 0.0003.
Values may be sent and summed in bfloat16 or wider, within the bound.
No kernel may reach another device: no remote copies, remote signals or barrier semaphores. Data moves between devices by JAX's collectives and lax.ppermute only.
A program may use at most 256 MiB of HBM per device.

```python
import math
import jax
import jax.numpy as jnp
from jax import lax

D = 2560
TOK_DEV = 1024
COLS = 2560
TOKENS = 131072
N_NODE = 8
N_FSDP = 16


def shared_mixing(key):
    return jax.random.truncated_normal(jax.random.fold_in(key, 101), -4.0, 4.0, (TOKENS,), jnp.float32)


def block_ramp(factor):
    block = jnp.arange(TOKENS) // TOK_DEV
    node_pos = (block // N_FSDP).astype(jnp.float32) / max(N_NODE - 1, 1)
    fsdp_pos = (block % N_FSDP).astype(jnp.float32) / max(N_FSDP - 1, 1)
    return jnp.exp(math.log(factor) * (node_pos + fsdp_pos))


def base_noise(key, count):
    return jax.random.truncated_normal(key, -4.0, 4.0, (TOKENS, count), jnp.float32)


def draw_activations(key, part):
    mixing = shared_mixing(key)
    key = jax.random.fold_in(key, 1)
    direction = jax.random.truncated_normal(jax.random.fold_in(key, 2), -4.0, 4.0, (D,), jnp.float32)
    feature_scale = jnp.exp(jax.random.uniform(jax.random.fold_in(key, 3), (D,), jnp.float32, math.log(0.3), math.log(3.0)))
    strength = float(TOK_DEV * N_FSDP) ** (-0.25)
    noise = base_noise(jax.random.fold_in(key, 4), D)
    values = noise + strength * mixing[:, None] * direction[None, :]
    return (values * feature_scale[None, :]).astype(jnp.bfloat16)


def draw_grad_out(key, part):
    mixing = shared_mixing(key)
    key = jax.random.fold_in(key, 2)
    direction = jax.random.truncated_normal(jax.random.fold_in(key, 5), -4.0, 4.0, (COLS,), jnp.float32)
    column_scale = jnp.exp(jax.random.uniform(jax.random.fold_in(key, 6), (COLS,), jnp.float32, math.log(0.3), math.log(3.0)))
    strength = float(TOK_DEV * N_FSDP) ** (-0.25)
    norm = 2.0 / math.sqrt(float(TOKENS))
    noise = base_noise(jax.random.fold_in(key, 7), COLS)
    ramp = block_ramp(3.0)
    values = noise + strength * mixing[:, None] * direction[None, :]
    return (values * column_scale[None, :] * (ramp * norm)[:, None]).astype(jnp.bfloat16)


def setup_inputs(seed: int = 0) -> dict:
    streams_of = jax.random.split(jax.random.key(seed), 3)
    activations = draw_activations(jax.random.fold_in(streams_of[2], 71), 0)
    grad_out = draw_grad_out(jax.random.fold_in(streams_of[2], 71), 0)
    return dict(activations=activations, grad_out=grad_out)


def node_gradient(x_node, dy_node):
    x_blocks = x_node.reshape(N_FSDP, TOK_DEV, D)
    dy_blocks = dy_node.reshape(N_FSDP, TOK_DEV, COLS)

    def accumulate(total, pair):
        product = lax.dot_general(pair[0], pair[1], (((0,), (0,)), ((), ())), preferred_element_type=jnp.float32)
        return total + product, None

    start = jnp.zeros((D, COLS), jnp.float32)
    total, _ = lax.scan(accumulate, start, (x_blocks, dy_blocks))
    return total


def reference(activations, grad_out):
    x_nodes = activations.reshape(N_NODE, N_FSDP * TOK_DEV, D)
    dy_nodes = grad_out.reshape(N_NODE, N_FSDP * TOK_DEV, COLS)
    vectors = lax.map(lambda pair: node_gradient(pair[0], pair[1]), (x_nodes, dy_nodes))
    levels = int(N_NODE).bit_length() - 1
    for level in range(levels):
        half = vectors.shape[0] // 2
        first = vectors[:half]
        second = vectors[half:]
        inner = jnp.sum(first * second, axis=(1, 2))
        first_sq = jnp.sum(first * first, axis=(1, 2))
        second_sq = jnp.sum(second * second, axis=(1, 2))
        coef_first = 1.0 - inner / (2.0 * (first_sq + 1e-6))
        coef_second = 1.0 - inner / (2.0 * (second_sq + 1e-6))
        vectors = coef_first[:, None, None] * first + coef_second[:, None, None] * second
    return vectors[0]
```

```python
import functools

import jax
import jax.numpy as jnp
from jax import lax
from jax.experimental import pallas as pl
from jax.experimental.pallas import tpu as pltpu
from jax.sharding import PartitionSpec as P

EPS = 1e-06
POWER = 17
TOP = 2.0 ** (124 / POWER)
TINY = 2.0**-126
PAD = 16
SIDE = 4
VMEM_BYTES = 60 * 2**20
BF16, F32 = jnp.bfloat16, jnp.float32


def encode(values):
    peak = jnp.max(jnp.abs(values), axis=0, keepdims=True).astype(BF16)
    x = values * (TOP / jnp.maximum(peak.astype(F32), TINY))
    x2 = x * x
    x4 = x2 * x2
    x8 = x4 * x4
    return (x8 * x8 * x).astype(BF16), peak


def decode(code, peak):
    code = code.astype(F32)
    size = jnp.exp(jnp.log(jnp.abs(code)) * (1.0 / POWER))
    return jnp.where(code < 0, -size, size) * (peak.astype(F32) * (1.0 / TOP))


def coordinates():
    node, fsdp = lax.axis_index("node"), lax.axis_index("fsdp")
    return lax.rem(fsdp, SIDE), node // 2, fsdp // SIDE, lax.rem(node, 2)


def masks(core):
    return 1 + 2 * core, 3 - 2 * core


def pairing(axis, first):
    pairs = []
    for y in range(SIDE):
        for core in range(2):
            mask = masks(core)[0 if first else 1]
            for z in range(SIDE):
                for x in range(SIDE):
                    at = dict(x=x, y=y, z=z)
                    to = dict(at)
                    to[axis] ^= mask
                    index = lambda p: (p["y"] * 2 + core) * SIDE * SIDE + p["z"] * SIDE + p["x"]
                    pairs.append((index(at), index(to)))
    return pairs


def exchange(array, axis, first):
    return lax.ppermute(array, ("node", "fsdp"), pairing(axis, first))


def block_offset(stream, p, q, rows):
    owner = jnp.where(stream == 0, q * SIDE + p, p * SIDE + q)
    return pl.multiple_of((owner * 2 + stream) * rows, 16)


def wanted(which, rows):
    x, _, z, core = coordinates()
    m1, m2 = masks(core)
    offsets = []
    for stream in range(2):
        p, q = (x, z) if stream == 0 else (z, x)
        everything = [q ^ 2, q ^ m1, q ^ m2, q]
        ps, qs = {
            "p1a": (p ^ 2, everything),
            "p1b": (p ^ m1, everything),
            "p2": (p ^ m2, everything),
            "q1": (p, everything[:2]),
            "q2": (p, everything[2:3]),
            "last": (p, everything[3:]),
        }[which]
        offsets.append([block_offset(stream, ps, each, rows) for each in qs])
    return offsets


def first_kernel(rows, x_ref, dy_ref, xt_ref, out0, out1, lhs):
    offsets = wanted("p1a", rows)
    count = len(offsets[0])

    @pl.when(pl.program_id(0) == 0)
    def _():
        for t in range(x_ref.shape[1] // 256):
            xt_ref[t * 256 : (t + 1) * 256, :] = x_ref[:, t * 256 : (t + 1) * 256].T
        for s in range(2):
            for b in range(count):
                at = (s * count + b) * rows
                lhs[at : at + rows, :] = xt_ref[pl.ds(offsets[s][b], rows), :]

    total = jnp.dot(lhs[...], dy_ref[...], preferred_element_type=F32)
    for s, out in enumerate((out0, out1)):
        code, peak = encode(total[s * count * rows : (s + 1) * count * rows])
        out[: count * rows, :] = code
        out[count * rows :, :] = jnp.broadcast_to(peak, (PAD, peak.shape[1]))


def fetch(xt_ref, lhs, sems, offsets, rows):
    copies = []
    for s in range(2):
        for b, offset in enumerate(offsets[s]):
            at = s * len(offsets[s]) + b
            copies.append(
                pltpu.make_async_copy(
                    xt_ref.at[pl.ds(offset, rows), :], lhs.at[pl.ds(at * rows, rows), :], sems.at[at]
                )
            )
    for copy in copies:
        copy.start()
    for copy in copies:
        copy.wait()


def step_kernel(which, rows, picks, xt_ref, dy_ref, *rest):
    arrivals, (out0, out1, lhs, sems) = rest[:-4], rest[-4:]
    offsets = wanted(which, rows)
    size = len(offsets[0]) * rows

    @pl.when(pl.program_id(0) == 0)
    def _():
        fetch(xt_ref, lhs, sems, offsets, rows)

    total = jnp.dot(lhs[...], dy_ref[...], preferred_element_type=F32)
    for s, out in enumerate((out0, out1)):
        part = total[s * size : (s + 1) * size]
        for k, pick in enumerate(picks):
            ref = arrivals[2 * k + s]
            scale = ref.shape[0] - PAD
            part += decode(ref[pick * rows : pick * rows + size, :], ref[scale : scale + 1, :])
        code, peak = encode(part)
        out[:size, :] = code
        out[size:, :] = jnp.broadcast_to(peak, (PAD, peak.shape[1]))


def step(which, rows, tile, xt, dy, arrivals, picks, count):
    tokens, cols = dy.shape
    size = count * rows
    message = jax.ShapeDtypeStruct((size + PAD, cols), BF16)
    column = lambda i: (0, i)
    return pl.pallas_call(
        functools.partial(step_kernel, which, rows, picks),
        grid=(cols // tile,),
        out_shape=[message, message],
        in_specs=[pl.BlockSpec(memory_space=pl.ANY), pl.BlockSpec((tokens, tile), column)]
        + [pl.BlockSpec((a.shape[0], tile), column) for a in arrivals],
        out_specs=[pl.BlockSpec((size + PAD, tile), column)] * 2,
        scratch_shapes=[pltpu.VMEM((2 * size, tokens), BF16), pltpu.SemaphoreType.DMA((2 * count,))],
        compiler_params=pltpu.CompilerParams(vmem_limit_bytes=VMEM_BYTES),
        name=which,
    )(xt, dy, *arrivals)


def first(rows, tile, x, dy):
    tokens, cols = dy.shape
    size = SIDE * rows
    message = jax.ShapeDtypeStruct((size + PAD, cols), BF16)
    column = lambda i: (0, i)
    return pl.pallas_call(
        functools.partial(first_kernel, rows),
        grid=(cols // tile,),
        out_shape=[jax.ShapeDtypeStruct((x.shape[1], tokens), BF16), message, message],
        in_specs=[pl.BlockSpec(x.shape, lambda i: (0, 0)), pl.BlockSpec((tokens, tile), column)],
        out_specs=[pl.BlockSpec((x.shape[1], tokens), lambda i: (0, 0))]
        + [pl.BlockSpec((size + PAD, tile), column)] * 2,
        scratch_shapes=[pltpu.VMEM((2 * size, tokens), BF16)],
        compiler_params=pltpu.CompilerParams(vmem_limit_bytes=VMEM_BYTES),
        name="p1a",
    )(x, dy)


def last_kernel(rows, picks, place, xt_ref, dy_ref, *rest):
    arrivals, (out0, out1, lhs, sems) = rest[:-4], rest[-4:]

    @pl.when(pl.program_id(0) == 0)
    def _():
        fetch(xt_ref, lhs, sems, wanted("last", rows), rows)

    total = jnp.dot(lhs[...], dy_ref[...], preferred_element_type=F32)
    parts = []
    for s in range(2):
        part = total[s * rows : (s + 1) * rows]
        for k, pick in enumerate(picks):
            ref = arrivals[2 * k + s]
            scale = ref.shape[0] - PAD
            part += decode(ref[pick * rows : (pick + 1) * rows, :], ref[scale : scale + 1, :])
        parts.append(part)
    code, peak = encode(jnp.concatenate(parts))

    def put(out):
        out[0, : 2 * rows, :] = code
        out[0, 2 * rows :, :] = jnp.broadcast_to(peak, (PAD, peak.shape[1]))

    pl.when(pl.program_id(0) < 2)(lambda: put(out0))
    pl.when(pl.program_id(0) >= 2)(lambda: put(out1))


def last(rows, place, xt, dy, arrivals, picks):
    tokens, cols = dy.shape
    tile = cols // SIDE
    message = jax.ShapeDtypeStruct((2, 2 * rows + PAD, tile), BF16)
    column = lambda i, place: (0, place[i])
    return pl.pallas_call(
        functools.partial(last_kernel, rows, picks),
        grid_spec=pltpu.PrefetchScalarGridSpec(
            num_scalar_prefetch=1,
            grid=(SIDE,),
            in_specs=[pl.BlockSpec(memory_space=pl.ANY), pl.BlockSpec((tokens, tile), column)]
            + [pl.BlockSpec((a.shape[0], tile), column) for a in arrivals],
            out_specs=[
                pl.BlockSpec((1, 2 * rows + PAD, tile), lambda i, place: (jnp.minimum(i, 1), 0, 0)),
                pl.BlockSpec((1, 2 * rows + PAD, tile), lambda i, place: (jnp.maximum(i, 2) - 2, 0, 0)),
            ],
            scratch_shapes=[pltpu.VMEM((2 * rows, tokens), BF16), pltpu.SemaphoreType.DMA((2,))],
        ),
        out_shape=[message, message],
        compiler_params=pltpu.CompilerParams(vmem_limit_bytes=VMEM_BYTES),
        name="last",
    )(place, xt, dy, *arrivals)


def gram_kernel(rows, half, y2own, y1arr, y2arr, carr, g_ref, gram_ref):
    _, y, _, core = coordinates()
    m1, m2 = masks(core)
    wide = g_ref.shape[2]
    lane = lax.broadcasted_iota(jnp.int32, (1, wide), 1)
    start = (wide - half) * core
    valid = (lane >= start) & (lane < start + half)
    at = pl.ds(pl.multiple_of((y2own.shape[2] - wide) * core, 128), wide)
    sources = [(y2own, 1, 0, 0), (y1arr, 1, m1, m2), (y2arr, 0, m2, m1), (y2arr, 1, 2, 2)]
    for k, (ref, index, mask, mask_other) in enumerate(sources):
        own = decode(ref[index, :rows, at], ref[index, rows : rows + 1, at])
        g_ref[(y ^ mask) * 2 + core] = jnp.where(valid, own, 0.0)
        other = decode(carr[k, :rows, :], carr[k, rows : rows + 1, :])
        g_ref[(y ^ mask_other) * 2 + 1 - core] = jnp.where(valid, other, 0.0)
    nodes = g_ref.shape[0]
    pairs = [(i, j) for i in range(nodes) for j in range(i, nodes)]

    def body(r, sums):
        blocks = [g_ref[n, pl.ds(r * 8, 8), :] for n in range(nodes)]
        out = []
        for total, (i, j) in zip(sums, pairs):
            product = blocks[i] * blocks[j]
            for t in range(wide // 128):
                total = total + product[:, t * 128 : (t + 1) * 128]
            out.append(total)
        return tuple(out)

    sums = lax.fori_loop(0, rows // 8, body, tuple(jnp.zeros((8, 128), F32) for _ in pairs))
    filled = [jnp.sum(total, axis=0, keepdims=True) for total in sums]
    filled += [jnp.zeros((1, 128), F32)] * (-len(pairs) % 8)
    stacked = jnp.sum(jnp.concatenate(filled), axis=1, keepdims=True)
    shape = (len(filled), 128)
    on = lax.broadcasted_iota(jnp.int32, shape, 0) == lax.broadcasted_iota(jnp.int32, shape, 1)
    row = jnp.sum(jnp.where(on, jnp.broadcast_to(stacked, shape), 0.0), axis=0, keepdims=True)
    gram_ref[...] = jnp.broadcast_to(row, gram_ref.shape)


def combine_kernel(half, g_ref, sums_ref, out_ref):
    nodes, rows, wide = g_ref.shape
    sums = jnp.sum(sums_ref[...], axis=0, keepdims=True)
    pairs = [(i, j) for i in range(nodes) for j in range(i, nodes)]
    gram = {}
    for k, (i, j) in enumerate(pairs):
        gram[i, j] = gram[j, i] = sums[:, k : k + 1]

    def inner(u, v):
        total = None
        for i, a in u.items():
            row = None
            for j, b in v.items():
                term = gram[i, j] * b
                row = term if row is None else row + term
            total = a * row if total is None else total + a * row
        return total

    one = jnp.ones((1, 1), F32)
    vectors = [{n: one} for n in range(nodes)]
    while len(vectors) > 1:
        middle = len(vectors) // 2
        merged = []
        for u, v in zip(vectors[:middle], vectors[middle:]):
            dot = inner(u, v)
            cu = 1.0 - dot / (2.0 * (inner(u, u) + EPS))
            cv = 1.0 - dot / (2.0 * (inner(v, v) + EPS))
            merged.append({**{n: cu * a for n, a in u.items()}, **{n: cv * a for n, a in v.items()}})
        vectors = merged
    total = None
    for n, coefficient in vectors[0].items():
        term = coefficient * g_ref[n]
        total = term if total is None else total + term
    core = lax.rem(lax.axis_index("node"), 2)
    moved = pltpu.roll(total, half, 1)
    out_ref[...] = jnp.where(core == 0, total[:, :half], moved[:, :half])


def local(x, dy):
    cols = dy.shape[1]
    rows = x.shape[1] // (2 * SIDE * SIDE)
    tile = cols // 5
    half = cols // (2 * SIDE)
    wide = -(-half // 128) * 128
    axes = ("x", "z")
    _, y, _, core = coordinates()
    m1, m2 = masks(core)
    place = jnp.stack([y ^ 2, y ^ m1, y ^ m2, y]).astype(jnp.int32)

    def send(pair, primary, is_first):
        return [exchange(m, axes[s] if primary else axes[1 - s], is_first) for s, m in enumerate(pair)]

    xt, *p1a = first(rows, tile, x, dy)
    p1a = send(p1a, True, True)
    p1b = send(step("p1b", rows, tile, xt, dy, [], [], 4), True, True)
    p2 = send(step("p2", rows, tile, xt, dy, p1a, [0], 4), True, False)
    q1 = send(step("q1", rows, tile, xt, dy, p1b + p2, [0, 0], 2), False, True)
    q2 = send(step("q2", rows, tile, xt, dy, p1b + p2 + q1, [2, 2, 0], 1), False, False)
    y1, y2 = last(rows, place, xt, dy, p1b + p2 + q1 + q2, [3, 3, 1, 0])
    y1arr = exchange(y1, "y", True)
    y2arr = exchange(jnp.stack([y2[0], y1arr[0]]), "y", False)
    across = jnp.stack([y2[1], y1arr[1], y2arr[0], y2arr[1]])
    start = (cols // SIDE - wide) * (1 - core)
    across = lax.dynamic_slice_in_dim(across, start, wide, axis=2)
    carr = lax.ppermute(across, "node", [(i, i ^ 1) for i in range(2 * SIDE)])
    params = pltpu.CompilerParams(vmem_limit_bytes=VMEM_BYTES)
    count = 2 * SIDE * SIDE * SIDE
    g, gram = pl.pallas_call(
        functools.partial(gram_kernel, 2 * rows, half),
        out_shape=[
            jax.ShapeDtypeStruct((2 * SIDE, 2 * rows, wide), F32),
            jax.ShapeDtypeStruct((count, 128), F32),
        ],
        compiler_params=params,
        name="gram",
    )(y2, y1arr, y2arr, carr)
    sums = lax.all_to_all(gram, ("node", "fsdp"), 0, 0, tiled=True)
    return pl.pallas_call(
        functools.partial(combine_kernel, half),
        out_shape=jax.ShapeDtypeStruct((2 * rows, half), F32),
        compiler_params=params,
        name="combine",
    )(g, sums)


def solution(mesh):
    in_specs = (P(("node", "fsdp"), None), P(("node", "fsdp"), None))
    out_specs = P("fsdp", "node")
    return jax.shard_map(local, mesh=mesh, in_specs=in_specs, out_specs=out_specs, check_vma=False)
```

```python
import functools

import jax
import jax.numpy as jnp
from jax import lax
from jax.experimental import pallas as pl
from jax.experimental.pallas import tpu as pltpu
from jax.sharding import PartitionSpec as P

EPS = 1e-06
POWER = 17
TOP = 2.0 ** (124 / POWER)
TINY = 2.0**-126
PAD = 8
SIDE = 4
BF16, F32 = jnp.bfloat16, jnp.float32


def encode(values):
    peak = jnp.max(jnp.abs(values), axis=0, keepdims=True).astype(BF16)
    x = values * (TOP / jnp.maximum(peak.astype(F32), TINY))
    x2 = x * x
    x4 = x2 * x2
    x8 = x4 * x4
    return (x8 * x8 * x).astype(BF16), peak


def decode(code, peak):
    code = code.astype(F32)
    size = jnp.exp(jnp.log(jnp.abs(code)) * (1.0 / POWER))
    return jnp.where(code < 0, -size, size) * (peak.astype(F32) * (1.0 / TOP))


def coordinates():
    node, fsdp = lax.axis_index("node"), lax.axis_index("fsdp")
    return lax.rem(fsdp, SIDE), node // 2, fsdp // SIDE, lax.rem(node, 2)


def masks(core):
    return 1 + 2 * core, 3 - 2 * core


def pairing(axis, first):
    pairs = []
    for y in range(SIDE):
        for core in range(2):
            mask = masks(core)[0 if first else 1]
            for z in range(SIDE):
                for x in range(SIDE):
                    at = dict(x=x, y=y, z=z)
                    to = dict(at)
                    to[axis] ^= mask
                    index = lambda p: (p["y"] * 2 + core) * SIDE * SIDE + p["z"] * SIDE + p["x"]
                    pairs.append((index(at), index(to)))
    return pairs


def exchange(array, axis, first):
    return lax.ppermute(array, ("node", "fsdp"), pairing(axis, first))


def block_offset(stream, p, q, rows):
    owner = jnp.where(stream == 0, q * SIDE + p, p * SIDE + q)
    return pl.multiple_of((owner * 2 + stream) * rows, 16)


def wanted(which, rows):
    x, _, z, core = coordinates()
    m1, m2 = masks(core)
    offsets = []
    for stream in range(2):
        p, q = (x, z) if stream == 0 else (z, x)
        everything = [q ^ 2, q ^ m1, q ^ m2, q]
        ps, qs = {
            "p1a_near": (p ^ 2, everything[:2]),
            "p1a_far": (p ^ 2, everything[2:]),
            "p1b_near": (p ^ m1, everything[:2]),
            "p1b_far": (p ^ m1, everything[2:]),
            "p2_near": (p ^ m2, everything[:2]),
            "p2_far": (p ^ m2, everything[2:]),
            "kept_near": (p, everything[:2]),
            "kept_far": (p, everything[2:]),
        }[which]
        offsets.append([block_offset(stream, ps, each, rows) for each in qs])
    return offsets


def gather(xt_ref, lhs, offsets, rows):
    for s in range(2):
        for b, offset in enumerate(offsets[s]):
            at = (s * len(offsets[s]) + b) * rows
            lhs[at : at + rows, :] = xt_ref[pl.ds(offset, rows), :]


def first_kernel(rows, tile, x_ref, dy_ref, xt_ref, dy_vmem, out0, out1, x_vmem, lhs, x_sems, dy_sems):
    x_cols, dy_cols = list(parts_of(x_ref, tile)), list(parts_of(dy_ref, tile))

    def bring(source, target, sems, cols):
        return [
            pltpu.make_async_copy(source.at[:, pl.ds(c.start, tile)], target.at[:, pl.ds(c.start, tile)], sems.at[t])
            for t, c in enumerate(cols)
        ]

    x_copies, dy_copies = bring(x_ref, x_vmem, x_sems, x_cols), bring(dy_ref, dy_vmem, dy_sems, dy_cols)
    for copy in x_copies + dy_copies:
        copy.start()
    for cols, copy in zip(x_cols, x_copies):
        copy.wait()
        xt_ref[cols, :] = x_vmem[:, cols].T
    gather(xt_ref, lhs, wanted("p1a_near", rows), rows)
    size = 2 * rows
    for cols, copy in zip(dy_cols, dy_copies):
        copy.wait()
        total = jnp.dot(lhs[...], dy_vmem[:, cols], preferred_element_type=F32)
        for s, out in enumerate((out0, out1)):
            write(out, total[s * size : (s + 1) * size], cols)


def product_kernel(which, rows, tile, coded, xt_ref, dy_ref, *rest):
    arrivals, (_, _, out0, out1, lhs) = rest[:-5], rest[-5:]
    offsets = wanted(which, rows)
    count = len(offsets[0])
    size = count * rows
    gather(xt_ref, lhs, offsets, rows)
    for cols in parts_of(dy_ref, tile):
        total = jnp.dot(lhs[...], dy_ref[:, cols], preferred_element_type=F32)
        for s, out in enumerate((out0, out1)):
            part = total[s * size : (s + 1) * size]
            for ref in arrivals[s::2]:
                part += read(ref, rows, 0, count, cols)
            if coded:
                write(out, part, cols)
            else:
                out[:, cols] = part


def params(mib):
    return pltpu.CompilerParams(vmem_limit_bytes=mib * 2**20)


def column(i):
    return (0, i)


VMEM = pl.BlockSpec(memory_space=pltpu.VMEM)


def product(which, rows, tile, count, xt, dy, arrivals, after, coded=True):
    tokens, cols = dy.shape
    size = count * rows
    message = jax.ShapeDtypeStruct((size + PAD if coded else size, cols), BF16 if coded else F32)
    return pl.pallas_call(
        functools.partial(product_kernel, which, rows, tile, coded),
        out_shape=[message, message],
        in_specs=[VMEM] * (2 + len(arrivals)) + [pl.BlockSpec(memory_space=pl.ANY)] * 2,
        out_specs=[VMEM] * 2,
        scratch_shapes=[pltpu.VMEM((2 * size, tokens), BF16)],
        compiler_params=params(12),
        name=which,
    )(xt, dy, *arrivals, *after)


def first(rows, tile, x, dy):
    tokens, cols = dy.shape
    size = 2 * rows
    message = jax.ShapeDtypeStruct((size + PAD, cols), BF16)
    xt = jax.ShapeDtypeStruct((x.shape[1], tokens), BF16)
    return pl.pallas_call(
        functools.partial(first_kernel, rows, tile),
        out_shape=[xt, jax.ShapeDtypeStruct(dy.shape, BF16), message, message],
        in_specs=[pl.BlockSpec(memory_space=pltpu.HBM)] * 2,
        out_specs=[VMEM] * 4,
        scratch_shapes=[
            pltpu.VMEM(x.shape, BF16),
            pltpu.VMEM((2 * size, tokens), BF16),
            pltpu.SemaphoreType.DMA((x.shape[1] // tile,)),
            pltpu.SemaphoreType.DMA((cols // tile,)),
        ],
        compiler_params=params(40),
        name="p1a_near",
    )(x, dy)


def parts_of(ref, tile):
    for at in range(0, ref.shape[1], tile):
        yield slice(at, at + tile)


def read(ref, rows, at, count, cols=slice(None)):
    scale = ref.shape[0] - PAD
    return decode(ref[at * rows : (at + count) * rows, cols], ref[scale : scale + 1, cols])


def write(out, values, cols=slice(None)):
    code, peak = encode(values)
    size = values.shape[0]
    out[:size, cols] = code
    out[size:, cols] = jnp.broadcast_to(peak, (PAD, peak.shape[1]))


def near_kernel(rows, tile, kept0, kept1, arr0, arr1, *rest):
    for kept, arr, out in ((kept0, arr0, rest[-2]), (kept1, arr1, rest[-1])):
        for cols in parts_of(kept, tile):
            write(out, kept[:rows, cols] + read(arr, rows, 0, 1, cols), cols)


def far_kernel(rows, tile, kept0, kept1, arr0, arr1, *rest):
    for kept, arr, out in ((kept0, arr0, rest[-2]), (kept1, arr1, rest[-1])):
        for cols in parts_of(kept, tile):
            write(out, kept[rows:, cols] + read(arr, rows, 1, 1, cols), cols)


def add_kernel(rows, tile, kept0, kept1, arr0, arr1, out0, out1):
    for kept, arr, out in ((kept0, arr0, out0), (kept1, arr1, out1)):
        for cols in parts_of(kept, tile):
            out[:, cols] = kept[:, cols] + read(arr, rows, 0, 2, cols)


def own_kernel(rows, tile, kept0, kept1, arr0, arr1, out):
    for s, (kept, arr) in enumerate(((kept0, arr0), (kept1, arr1))):
        for cols in parts_of(kept, tile):
            out[s * rows : (s + 1) * rows, cols] = kept[rows:, cols] + read(arr, rows, 0, 1, cols)


def merge(name, kernel, rows, tile, ins, heights, outs, after=()):
    cols = ins[0].shape[1]
    return pl.pallas_call(
        functools.partial(kernel, rows, tile),
        out_shape=[jax.ShapeDtypeStruct((h, cols), dtype) for h, dtype in zip(heights, outs)],
        in_specs=[VMEM] * len(ins) + [pl.BlockSpec(memory_space=pl.ANY)] * len(after),
        out_specs=[VMEM] * len(outs),
        compiler_params=params(12),
        name=name,
    )(*ins, *after)


def last_kernel(rows, place, own, arr0, arr1, out0, out1, out2, out3):
    values = jnp.concatenate([own[s * rows : (s + 1) * rows, :] + read(a, rows, 0, 1) for s, a in enumerate((arr0, arr1))])
    for k, out in enumerate((out0, out1, out2, out3)):
        pl.when(pl.program_id(0) == k)(functools.partial(write, out, values))


def last(rows, place, own, arrivals):
    cols = own.shape[1]
    tile = cols // SIDE
    height = 2 * rows + PAD
    at = lambda i, place: (0, place[i])
    return pl.pallas_call(
        functools.partial(last_kernel, rows),
        grid_spec=pltpu.PrefetchScalarGridSpec(
            num_scalar_prefetch=1,
            grid=(SIDE,),
            in_specs=[pl.BlockSpec((2 * rows, tile), at)] + [pl.BlockSpec((a.shape[0], tile), at) for a in arrivals],
            out_specs=[pl.BlockSpec((height, tile), lambda i, place: (0, 0))] * SIDE,
        ),
        out_shape=[jax.ShapeDtypeStruct((height, tile), BF16)] * SIDE,
        compiler_params=params(12),
        name="last",
    )(place, own, *arrivals)


def gram_kernel(rows, half, own0, own1, own2, own3, carr, g_ref, gram_ref):
    _, y, _, core = coordinates()
    m1, m2 = masks(core)
    wide = g_ref.shape[2]
    lane = lax.broadcasted_iota(jnp.int32, (1, wide), 1)
    start = (wide - half) * core
    valid = (lane >= start) & (lane < start + half)
    at = pl.ds(pl.multiple_of((own0.shape[1] - wide) * core, 128), wide)
    sources = [(own0, 0, 0), (own1, m1, m2), (own2, m2, m1), (own3, 2, 2)]
    for k, (ref, mask, mask_other) in enumerate(sources):
        own = decode(ref[:rows, at], ref[rows : rows + 1, at])
        g_ref[(y ^ mask) * 2 + core] = jnp.where(valid, own, 0.0)
        other = decode(carr[k, :rows, :], carr[k, rows : rows + 1, :])
        g_ref[(y ^ mask_other) * 2 + 1 - core] = jnp.where(valid, other, 0.0)
    nodes = g_ref.shape[0]
    pairs = [(i, j) for i in range(nodes) for j in range(i, nodes)]

    def body(r, sums):
        blocks = [g_ref[n, pl.ds(r * 8, 8), :] for n in range(nodes)]
        out = []
        for total, (i, j) in zip(sums, pairs):
            product = blocks[i] * blocks[j]
            for t in range(wide // 128):
                total = total + product[:, t * 128 : (t + 1) * 128]
            out.append(total)
        return tuple(out)

    sums = lax.fori_loop(0, rows // 8, body, tuple(jnp.zeros((8, 128), F32) for _ in pairs))
    filled = [jnp.sum(total, axis=0, keepdims=True) for total in sums]
    filled += [jnp.zeros((1, 128), F32)] * (-len(pairs) % 8)
    stacked = jnp.sum(jnp.concatenate(filled), axis=1, keepdims=True)
    shape = (len(filled), 128)
    on = lax.broadcasted_iota(jnp.int32, shape, 0) == lax.broadcasted_iota(jnp.int32, shape, 1)
    row = jnp.sum(jnp.where(on, jnp.broadcast_to(stacked, shape), 0.0), axis=0, keepdims=True)
    gram_ref[...] = jnp.broadcast_to(row, gram_ref.shape)


def combine_kernel(half, g_ref, sums_ref, out_ref):
    nodes, rows, wide = g_ref.shape
    sums = jnp.sum(sums_ref[...], axis=0, keepdims=True)
    pairs = [(i, j) for i in range(nodes) for j in range(i, nodes)]
    gram = {}
    for k, (i, j) in enumerate(pairs):
        gram[i, j] = gram[j, i] = sums[:, k : k + 1]

    def inner(u, v):
        total = None
        for i, a in u.items():
            row = None
            for j, b in v.items():
                term = gram[i, j] * b
                row = term if row is None else row + term
            total = a * row if total is None else total + a * row
        return total

    one = jnp.ones((1, 1), F32)
    vectors = [{n: one} for n in range(nodes)]
    while len(vectors) > 1:
        middle = len(vectors) // 2
        merged = []
        for u, v in zip(vectors[:middle], vectors[middle:]):
            dot = inner(u, v)
            cu = 1.0 - dot / (2.0 * (inner(u, u) + EPS))
            cv = 1.0 - dot / (2.0 * (inner(v, v) + EPS))
            merged.append({**{n: cu * a for n, a in u.items()}, **{n: cv * a for n, a in v.items()}})
        vectors = merged
    total = None
    for n, coefficient in vectors[0].items():
        term = coefficient * g_ref[n]
        total = term if total is None else total + term
    core = lax.rem(lax.axis_index("node"), 2)
    moved = pltpu.roll(total, half, 1)
    out_ref[...] = jnp.where(core == 0, total[:, :half], moved[:, :half])


def local(x, dy):
    cols = dy.shape[1]
    rows = x.shape[1] // (2 * SIDE * SIDE)
    half = cols // (2 * SIDE)
    wide = -(-half // 128) * 128
    axes = ("x", "z")
    _, y, _, core = coordinates()
    m1, m2 = masks(core)
    place = jnp.stack([y ^ 2, y ^ m1, y ^ m2, y]).astype(jnp.int32)

    def send(pair, primary, is_first):
        return [exchange(m, axes[s] if primary else axes[1 - s], is_first) for s, m in enumerate(pair)]

    make = functools.partial(product, rows=rows, tile=256, count=2)
    xt, dyv, *m1 = first(rows, 256, x, dy)
    p1a_near = send(m1, True, True)
    p1a_far = send(make("p1a_far", xt=xt, dy=dyv, arrivals=[], after=m1), True, True)
    p1b_near = send(make("p1b_near", xt=xt, dy=dyv, arrivals=[], after=p1a_near), True, True)
    p2_near = send(make("p2_near", xt=xt, dy=dyv, arrivals=p1a_near, after=p1a_far), True, False)
    p1b_far = send(make("p1b_far", xt=xt, dy=dyv, arrivals=[], after=p1b_near), True, True)
    p2_far = send(make("p2_far", xt=xt, dy=dyv, arrivals=p1a_far, after=p2_near), True, False)
    kept_near = make("kept_near", xt=xt, dy=dyv, arrivals=p1b_near, after=p1b_near, coded=False)
    kept_far = make("kept_far", xt=xt, dy=dyv, arrivals=p1b_far, after=p1b_far, coded=False)
    one = [rows + PAD] * 2
    two = [2 * rows] * 2
    q1_near = send(merge("q1_near", near_kernel, rows, 256, [*kept_near, *p2_near], one, [BF16] * 2, p1b_far), False, True)
    q1_far = send(merge("q1_far", far_kernel, rows, 256, [*kept_near, *p2_near], one, [BF16] * 2, p2_far), False, True)
    rest = merge("rest", add_kernel, rows, 256, [*kept_far, *p2_far], two, [F32] * 2)
    q2 = send(merge("q2", near_kernel, rows, 256, [*rest, *q1_near], one, [BF16] * 2), False, False)
    own = merge("own", own_kernel, rows, 256, [*rest, *q1_far], two[:1], [F32])
    far, near1, near2, mine = last(rows, place, own[0], q2)
    far = lax.ppermute(far, "node", [(i, i ^ 4) for i in range(2 * SIDE)])
    near1 = exchange(near1, "y", True)
    near2 = exchange(near2, "y", False)
    blocks = [mine, near1, near2, far]
    start = (cols // SIDE - wide) * (1 - core)
    across = jnp.stack([lax.dynamic_slice_in_dim(b, start, wide, axis=1) for b in blocks])
    carr = lax.ppermute(across, "node", [(i, i ^ 1) for i in range(2 * SIDE)])
    count = 2 * SIDE * SIDE * SIDE
    g, gram = pl.pallas_call(
        functools.partial(gram_kernel, 2 * rows, half),
        out_shape=[
            jax.ShapeDtypeStruct((2 * SIDE, 2 * rows, wide), F32),
            jax.ShapeDtypeStruct((count, 128), F32),
        ],
        compiler_params=params(12),
        name="gram",
    )(*blocks, carr)
    sums = lax.all_to_all(gram, ("node", "fsdp"), 0, 0, tiled=True)
    return pl.pallas_call(
        functools.partial(combine_kernel, half),
        out_shape=jax.ShapeDtypeStruct((2 * rows, half), F32),
        compiler_params=params(12),
        name="combine",
    )(g, sums)


def solution(mesh):
    in_specs = (P(("node", "fsdp"), None), P(("node", "fsdp"), None))
    out_specs = P("fsdp", "node")
    return jax.shard_map(local, mesh=mesh, in_specs=in_specs, out_specs=out_specs, check_vma=False)
```

```python
import functools

import jax
import jax.numpy as jnp
from jax import lax
from jax.experimental import pallas as pl
from jax.experimental.pallas import tpu as pltpu
from jax.sharding import PartitionSpec as P

EPS = 1e-06
POWER = 17
TOP = 2.0 ** (124 / POWER)
TINY = 2.0**-126
PAD = 8
SIDE = 4
BF16, F32 = jnp.bfloat16, jnp.float32


def encode(values):
    peak = jnp.max(jnp.abs(values), axis=0, keepdims=True).astype(BF16)
    x = values * (TOP / jnp.maximum(peak.astype(F32), TINY))
    x2 = x * x
    x4 = x2 * x2
    x8 = x4 * x4
    return (x8 * x8 * x).astype(BF16), peak


def decode(code, peak):
    code = code.astype(F32)
    size = jnp.exp(jnp.log(jnp.abs(code)) * (1.0 / POWER))
    return jnp.where(code < 0, -size, size) * (peak.astype(F32) * (1.0 / TOP))


def coordinates():
    node, fsdp = lax.axis_index("node"), lax.axis_index("fsdp")
    return lax.rem(fsdp, SIDE), node // 2, fsdp // SIDE, lax.rem(node, 2)


def masks(core):
    return 1 + 2 * core, 3 - 2 * core


def pairing(axis, first):
    pairs = []
    for y in range(SIDE):
        for core in range(2):
            mask = masks(core)[0 if first else 1]
            for z in range(SIDE):
                for x in range(SIDE):
                    at = dict(x=x, y=y, z=z)
                    to = dict(at)
                    to[axis] ^= mask
                    index = lambda p: (p["y"] * 2 + core) * SIDE * SIDE + p["z"] * SIDE + p["x"]
                    pairs.append((index(at), index(to)))
    return pairs


def exchange(array, axis, first):
    return lax.ppermute(array, ("node", "fsdp"), pairing(axis, first))


def block_offset(stream, p, q, rows):
    owner = jnp.where(stream == 0, q * SIDE + p, p * SIDE + q)
    return pl.multiple_of((owner * 2 + stream) * rows, 16)


def wanted(which, rows):
    x, _, z, core = coordinates()
    m1, m2 = masks(core)
    offsets = []
    for stream in range(2):
        p, q = (x, z) if stream == 0 else (z, x)
        everything = [q ^ 2, q ^ m1, q ^ m2, q]
        ps, qs = {
            "p1a_near": (p ^ 2, everything[:2]),
            "p1a_far": (p ^ 2, everything[2:]),
            "p1b_near": (p ^ m1, everything[:2]),
            "p1b_far": (p ^ m1, everything[2:]),
            "p2_near": (p ^ m2, everything[:2]),
            "p2_far": (p ^ m2, everything[2:]),
            "kept_near": (p, everything[:2]),
            "kept_far": (p, everything[2:]),
        }[which]
        offsets.append([block_offset(stream, ps, each, rows) for each in qs])
    return offsets


def gather(xt_ref, lhs, offsets, rows):
    for s in range(2):
        for b, offset in enumerate(offsets[s]):
            at = (s * len(offsets[s]) + b) * rows
            lhs[at : at + rows, :] = xt_ref[pl.ds(offset, rows), :]


def first_kernel(rows, tile, x_ref, dy_ref, xt_ref, dy_vmem, out0, out1, x_vmem, lhs, x_sems, dy_sems):
    x_rows = [pl.ds(at, tile) for at in range(0, x_ref.shape[0], tile)]
    dy_cols = [pl.ds(at, 2 * tile) for at in range(0, dy_ref.shape[1], 2 * tile)]
    x_copies = [pltpu.make_async_copy(x_ref.at[r, :], x_vmem.at[r, :], x_sems.at[t]) for t, r in enumerate(x_rows)]
    dy_copies = [pltpu.make_async_copy(dy_ref.at[:, c], dy_vmem.at[:, c], dy_sems.at[t]) for t, c in enumerate(dy_cols)]
    for copy in x_copies + dy_copies:
        copy.start()
    for at, copy in zip(range(0, x_ref.shape[0], tile), x_copies):
        copy.wait()
        for cols in parts_of(x_ref, tile):
            xt_ref[cols, at : at + tile] = x_vmem[at : at + tile, cols].T
    gather(xt_ref, lhs, wanted("p1a_near", rows), rows)
    size = 2 * rows
    for t, copy in enumerate(dy_copies):
        copy.wait()
        for cols in (slice(2 * t * tile, (2 * t + 1) * tile), slice((2 * t + 1) * tile, (2 * t + 2) * tile)):
            total = jnp.dot(lhs[...], dy_vmem[:, cols], preferred_element_type=F32)
            for s, out in enumerate((out0, out1)):
                write(out, total[s * size : (s + 1) * size], cols)


def product_kernel(which, rows, tile, coded, xt_ref, dy_ref, *rest):
    arrivals, (_, _, out0, out1, lhs) = rest[:-5], rest[-5:]
    offsets = wanted(which, rows)
    count = len(offsets[0])
    size = count * rows
    gather(xt_ref, lhs, offsets, rows)
    for cols in parts_of(dy_ref, tile):
        total = jnp.dot(lhs[...], dy_ref[:, cols], preferred_element_type=F32)
        for s, out in enumerate((out0, out1)):
            part = total[s * size : (s + 1) * size]
            for ref in arrivals[s::2]:
                part += read(ref, rows, 0, count, cols)
            if coded:
                write(out, part, cols)
            else:
                out[:, cols] = part


def params(mib):
    return pltpu.CompilerParams(vmem_limit_bytes=mib * 2**20)


def column(i):
    return (0, i)


VMEM = pl.BlockSpec(memory_space=pltpu.VMEM)


def product(which, rows, tile, count, xt, dy, arrivals, after, coded=True):
    tokens, cols = dy.shape
    size = count * rows
    message = jax.ShapeDtypeStruct((size + PAD if coded else size, cols), BF16 if coded else F32)
    return pl.pallas_call(
        functools.partial(product_kernel, which, rows, tile, coded),
        out_shape=[message, message],
        in_specs=[VMEM] * (2 + len(arrivals)) + [pl.BlockSpec(memory_space=pl.ANY)] * 2,
        out_specs=[VMEM] * 2,
        scratch_shapes=[pltpu.VMEM((2 * size, tokens), BF16)],
        compiler_params=params(12),
        name=which,
    )(xt, dy, *arrivals, *after)


def first(rows, tile, x, dy):
    tokens, cols = dy.shape
    size = 2 * rows
    message = jax.ShapeDtypeStruct((size + PAD, cols), BF16)
    xt = jax.ShapeDtypeStruct((x.shape[1], tokens), BF16)
    return pl.pallas_call(
        functools.partial(first_kernel, rows, tile),
        out_shape=[xt, jax.ShapeDtypeStruct(dy.shape, BF16), message, message],
        in_specs=[pl.BlockSpec(memory_space=pltpu.HBM)] * 2,
        out_specs=[VMEM] * 4,
        scratch_shapes=[
            pltpu.VMEM(x.shape, BF16),
            pltpu.VMEM((2 * size, tokens), BF16),
            pltpu.SemaphoreType.DMA((tokens // tile,)),
            pltpu.SemaphoreType.DMA((cols // (2 * tile),)),
        ],
        compiler_params=params(40),
        name="p1a_near",
    )(x, dy)


def parts_of(ref, tile):
    for at in range(0, ref.shape[1], tile):
        yield slice(at, at + tile)


def read(ref, rows, at, count, cols=slice(None)):
    scale = ref.shape[0] - PAD
    return decode(ref[at * rows : (at + count) * rows, cols], ref[scale : scale + 1, cols])


def write(out, values, cols=slice(None)):
    code, peak = encode(values)
    size = values.shape[0]
    out[:size, cols] = code
    out[size:, cols] = jnp.broadcast_to(peak, (PAD, peak.shape[1]))


def near_kernel(rows, tile, kept0, kept1, arr0, arr1, *rest):
    for kept, arr, out in ((kept0, arr0, rest[-2]), (kept1, arr1, rest[-1])):
        for cols in parts_of(kept, tile):
            write(out, kept[:rows, cols] + read(arr, rows, 0, 1, cols), cols)


def far_kernel(rows, tile, kept0, kept1, arr0, arr1, *rest):
    for kept, arr, out in ((kept0, arr0, rest[-2]), (kept1, arr1, rest[-1])):
        for cols in parts_of(kept, tile):
            write(out, kept[rows:, cols] + read(arr, rows, 1, 1, cols), cols)


def add_kernel(rows, tile, kept0, kept1, arr0, arr1, out0, out1):
    for kept, arr, out in ((kept0, arr0, out0), (kept1, arr1, out1)):
        for cols in parts_of(kept, tile):
            out[:, cols] = kept[:, cols] + read(arr, rows, 0, 2, cols)


def own_kernel(rows, tile, kept0, kept1, arr0, arr1, out):
    for s, (kept, arr) in enumerate(((kept0, arr0), (kept1, arr1))):
        for cols in parts_of(kept, tile):
            out[s * rows : (s + 1) * rows, cols] = kept[rows:, cols] + read(arr, rows, 0, 1, cols)


def merge(name, kernel, rows, tile, ins, heights, outs, after=()):
    cols = ins[0].shape[1]
    return pl.pallas_call(
        functools.partial(kernel, rows, tile),
        out_shape=[jax.ShapeDtypeStruct((h, cols), dtype) for h, dtype in zip(heights, outs)],
        in_specs=[VMEM] * len(ins) + [pl.BlockSpec(memory_space=pl.ANY)] * len(after),
        out_specs=[VMEM] * len(outs),
        compiler_params=params(12),
        name=name,
    )(*ins, *after)


def last_kernel(rows, own, arr0, arr1, *outs):
    _, y, _, core = coordinates()
    m1, m2 = masks(core)
    width = own.shape[1] // SIDE
    for out, at in zip(outs, (y ^ 2, y ^ m1, y ^ m2, y)):
        cols = pl.ds(pl.multiple_of(at * width, 128), width)
        parts = [own[s * rows : (s + 1) * rows, cols] + read(a, rows, 0, 1, cols) for s, a in enumerate((arr0, arr1))]
        write(out, jnp.concatenate(parts))


def last(rows, own, arrivals):
    message = jax.ShapeDtypeStruct((2 * rows + PAD, own.shape[1] // SIDE), BF16)
    return pl.pallas_call(
        functools.partial(last_kernel, rows),
        out_shape=[message] * SIDE,
        in_specs=[VMEM] * 3,
        out_specs=[VMEM] * SIDE,
        compiler_params=params(12),
        name="last",
    )(own, *arrivals)


def gram_kernel(rows, half, own0, own1, own2, own3, carr, g_ref, gram_ref):
    _, y, _, core = coordinates()
    m1, m2 = masks(core)
    wide = g_ref.shape[2]
    lane = lax.broadcasted_iota(jnp.int32, (1, wide), 1)
    start = (wide - half) * core
    valid = (lane >= start) & (lane < start + half)
    at = pl.ds(pl.multiple_of((own0.shape[1] - wide) * core, 128), wide)
    sources = [(own0, 0, 0), (own1, m1, m2), (own2, m2, m1), (own3, 2, 2)]
    for k, (ref, mask, mask_other) in enumerate(sources):
        own = decode(ref[:rows, at], ref[rows : rows + 1, at])
        g_ref[(y ^ mask) * 2 + core] = jnp.where(valid, own, 0.0)
        other = decode(carr[k, :rows, :], carr[k, rows : rows + 1, :])
        g_ref[(y ^ mask_other) * 2 + 1 - core] = jnp.where(valid, other, 0.0)
    nodes = g_ref.shape[0]
    pairs = [(i, j) for i in range(nodes) for j in range(i, nodes)]

    def body(r, sums):
        blocks = [g_ref[n, pl.ds(r * 8, 8), :] for n in range(nodes)]
        out = []
        for total, (i, j) in zip(sums, pairs):
            product = blocks[i] * blocks[j]
            for t in range(wide // 128):
                total = total + product[:, t * 128 : (t + 1) * 128]
            out.append(total)
        return tuple(out)

    sums = lax.fori_loop(0, rows // 8, body, tuple(jnp.zeros((8, 128), F32) for _ in pairs))
    filled = [jnp.sum(total, axis=0, keepdims=True) for total in sums]
    filled += [jnp.zeros((1, 128), F32)] * (-len(pairs) % 8)
    stacked = jnp.sum(jnp.concatenate(filled), axis=1, keepdims=True)
    shape = (len(filled), 128)
    on = lax.broadcasted_iota(jnp.int32, shape, 0) == lax.broadcasted_iota(jnp.int32, shape, 1)
    row = jnp.sum(jnp.where(on, jnp.broadcast_to(stacked, shape), 0.0), axis=0, keepdims=True)
    gram_ref[...] = jnp.broadcast_to(row, gram_ref.shape)


def combine_kernel(half, g_ref, sums_ref, out_ref):
    nodes, rows, wide = g_ref.shape
    sums = jnp.sum(sums_ref[...], axis=0, keepdims=True)
    pairs = [(i, j) for i in range(nodes) for j in range(i, nodes)]
    gram = {}
    for k, (i, j) in enumerate(pairs):
        gram[i, j] = gram[j, i] = sums[:, k : k + 1]

    def inner(u, v):
        total = None
        for i, a in u.items():
            row = None
            for j, b in v.items():
                term = gram[i, j] * b
                row = term if row is None else row + term
            total = a * row if total is None else total + a * row
        return total

    one = jnp.ones((1, 1), F32)
    vectors = [{n: one} for n in range(nodes)]
    while len(vectors) > 1:
        middle = len(vectors) // 2
        merged = []
        for u, v in zip(vectors[:middle], vectors[middle:]):
            dot = inner(u, v)
            cu = 1.0 - dot / (2.0 * (inner(u, u) + EPS))
            cv = 1.0 - dot / (2.0 * (inner(v, v) + EPS))
            merged.append({**{n: cu * a for n, a in u.items()}, **{n: cv * a for n, a in v.items()}})
        vectors = merged
    total = None
    for n, coefficient in vectors[0].items():
        term = coefficient * g_ref[n]
        total = term if total is None else total + term
    core = lax.rem(lax.axis_index("node"), 2)
    moved = pltpu.roll(total, half, 1)
    out_ref[...] = jnp.where(core == 0, total[:, :half], moved[:, :half])


def local(x, dy):
    cols = dy.shape[1]
    rows = x.shape[1] // (2 * SIDE * SIDE)
    half = cols // (2 * SIDE)
    wide = -(-half // 128) * 128
    axes = ("x", "z")
    core = coordinates()[3]

    def send(pair, primary, is_first):
        return [exchange(m, axes[s] if primary else axes[1 - s], is_first) for s, m in enumerate(pair)]

    make = functools.partial(product, rows=rows, tile=256, count=2)
    xt, dyv, *m1 = first(rows, 256, x, dy)
    p1a_near = send(m1, True, True)
    m2 = make("p1a_far", xt=xt, dy=dyv, arrivals=[], after=m1)
    p1a_far = send(m2, True, True)
    p1b_near = send(make("p1b_near", xt=xt, dy=dyv, arrivals=[], after=m2), True, True)
    p2_near = send(make("p2_near", xt=xt, dy=dyv, arrivals=p1a_near, after=p1a_near), True, False)
    p1b_far = send(make("p1b_far", xt=xt, dy=dyv, arrivals=[], after=p1a_far), True, True)
    p2_far = send(make("p2_far", xt=xt, dy=dyv, arrivals=p1a_far, after=p1b_near), True, False)
    kept_near = make("kept_near", xt=xt, dy=dyv, arrivals=p1b_near, after=p1b_near, coded=False)
    kept_far = make("kept_far", xt=xt, dy=dyv, arrivals=p1b_far, after=p1b_far, coded=False)
    one = [rows + PAD] * 2
    two = [2 * rows] * 2
    q1_near = send(merge("q1_near", near_kernel, rows, 256, [*kept_near, *p2_near], one, [BF16] * 2), False, True)
    q1_far = send(merge("q1_far", far_kernel, rows, 256, [*kept_near, *p2_near], one, [BF16] * 2, p1b_far), False, True)
    rest = merge("rest", add_kernel, rows, 256, [*kept_far, *p2_far], two, [F32] * 2)
    q2 = send(merge("q2", near_kernel, rows, 256, [*rest, *q1_near], one, [BF16] * 2), False, False)
    own = merge("own", own_kernel, rows, 256, [*rest, *q1_far], two[:1], [F32])
    far, near1, near2, mine = last(rows, own[0], q2)
    far = lax.ppermute(far, "node", [(i, i ^ 4) for i in range(2 * SIDE)])
    near1 = exchange(near1, "y", True)
    near2 = exchange(near2, "y", False)
    blocks = [mine, near1, near2, far]
    start = (cols // SIDE - wide) * (1 - core)
    across = jnp.stack([lax.dynamic_slice_in_dim(b, start, wide, axis=1) for b in blocks])
    carr = lax.ppermute(across, "node", [(i, i ^ 1) for i in range(2 * SIDE)])
    count = 2 * SIDE * SIDE * SIDE
    g, gram = pl.pallas_call(
        functools.partial(gram_kernel, 2 * rows, half),
        out_shape=[
            jax.ShapeDtypeStruct((2 * SIDE, 2 * rows, wide), F32),
            jax.ShapeDtypeStruct((count, 128), F32),
        ],
        compiler_params=params(12),
        name="gram",
    )(*blocks, carr)
    sums = lax.all_to_all(gram, ("node", "fsdp"), 0, 0, tiled=True)
    return pl.pallas_call(
        functools.partial(combine_kernel, half),
        out_shape=jax.ShapeDtypeStruct((2 * rows, half), F32),
        compiler_params=params(12),
        name="combine",
    )(g, sums)


def solution(mesh):
    in_specs = (P(("node", "fsdp"), None), P(("node", "fsdp"), None))
    out_specs = P("fsdp", "node")
    return jax.shard_map(local, mesh=mesh, in_specs=in_specs, out_specs=out_specs, check_vma=False)
```

```python
import functools

import jax
import jax.numpy as jnp
from jax import lax
from jax.experimental import pallas as pl
from jax.experimental.pallas import tpu as pltpu
from jax.sharding import PartitionSpec as P

EPS = 1e-06
POWER = 17
TOP = 2.0 ** (124 / POWER)
TINY = 2.0**-126
LANES = 128
WIDE_ROWS = 8
GROUP = 16
SIDE = 4
BF16, F32 = jnp.bfloat16, jnp.float32


def encode(values):
    peak = jnp.max(jnp.abs(values), axis=0, keepdims=True).astype(BF16).astype(F32)
    x = values * (TOP / jnp.maximum(peak, TINY))
    x2 = x * x
    x4 = x2 * x2
    x8 = x4 * x4
    return (x8 * x8 * x).astype(BF16), peak


def decode(code, peak):
    code = code.astype(F32)
    size = jnp.exp(jnp.log(jnp.abs(code)) * (1.0 / POWER))
    return jnp.where(code < 0, -size, size) * (peak * (1.0 / TOP))


def scale_rows(tiles):
    return -(-tiles // GROUP) * GROUP


def message(rows, cols, wide=False):
    tiles = cols // LANES
    if wide:
        return jax.ShapeDtypeStruct((rows + WIDE_ROWS, cols), BF16)
    return jax.ShapeDtypeStruct((tiles * rows + scale_rows(tiles), LANES), BF16)


class Reader:
    def __init__(self, ref, cols, rows):
        self.ref, self.rows = ref, rows
        tiles = cols // LANES
        self.wide = ref.shape[1] == cols
        if self.wide:
            self.height = ref.shape[0] - WIDE_ROWS
            return
        self.height = (ref.shape[0] - scale_rows(tiles)) // tiles
        self.scales = ref[tiles * self.height :, :].astype(F32)

    def __call__(self, at, count, cols):
        if self.wide:
            values = self.ref[at * self.rows : (at + count) * self.rows, cols]
            return decode(values, self.ref[self.height : self.height + 1, cols].astype(F32))
        out = []
        for t in range(cols.start // LANES, cols.stop // LANES):
            first = t * self.height + at * self.rows
            out.append(decode(self.ref[first : first + count * self.rows, :], self.scales[t : t + 1]))
        return jnp.concatenate(out, axis=1)

    def dynamic(self, tile):
        if self.wide:
            cols = pl.ds(pl.multiple_of(tile * LANES, LANES), LANES)
            return decode(self.ref[: self.height, cols], self.ref[self.height : self.height + 1, cols].astype(F32))
        on = lax.broadcasted_iota(jnp.int32, self.scales.shape, 0) == tile
        peak = jnp.sum(jnp.where(on, self.scales, 0.0), axis=0, keepdims=True)
        first = pl.multiple_of(tile * self.height, GROUP)
        return decode(self.ref[pl.ds(first, self.height), :], peak)


class Writer:
    def __init__(self, out):
        self.out, self.at, self.peaks = out, 0, []

    def __call__(self, values):
        code, peak = encode(values)
        rows, width = values.shape
        if self.out.shape[1] > LANES:
            cols = slice(self.at, self.at + width)
            self.out[:rows, cols] = code
            self.out[rows:, cols] = jnp.broadcast_to(peak, (WIDE_ROWS, width)).astype(BF16)
            self.at += width
            return
        for t in range(0, values.shape[1], LANES):
            self.out[self.at : self.at + rows, :] = code[:, t : t + LANES]
            self.at += rows
            self.peaks.append(peak[:, t : t + LANES])

    def close(self):
        if self.out.shape[1] > LANES:
            return
        spare = [jnp.zeros((1, LANES), F32)] * (scale_rows(len(self.peaks)) - len(self.peaks))
        self.out[self.at :, :] = jnp.concatenate(self.peaks + spare).astype(BF16)


def coordinates():
    node, fsdp = lax.axis_index("node"), lax.axis_index("fsdp")
    return lax.rem(fsdp, SIDE), node // 2, fsdp // SIDE, lax.rem(node, 2)


def masks(core):
    return 1 + 2 * core, 3 - 2 * core


def pairing(axis, first):
    pairs = []
    for y in range(SIDE):
        for core in range(2):
            mask = masks(core)[0 if first else 1]
            for z in range(SIDE):
                for x in range(SIDE):
                    at = dict(x=x, y=y, z=z)
                    to = dict(at)
                    to[axis] ^= mask
                    index = lambda p: (p["y"] * 2 + core) * SIDE * SIDE + p["z"] * SIDE + p["x"]
                    pairs.append((index(at), index(to)))
    return pairs


def exchange(array, axis, first):
    return lax.ppermute(array, ("node", "fsdp"), pairing(axis, first))


def block_offset(stream, p, q, rows):
    owner = jnp.where(stream == 0, q * SIDE + p, p * SIDE + q)
    return pl.multiple_of((owner * 2 + stream) * rows, 16)


def wanted(which, rows):
    x, _, z, core = coordinates()
    m1, m2 = masks(core)
    offsets = []
    for stream in range(2):
        p, q = (x, z) if stream == 0 else (z, x)
        everything = [q ^ 2, q ^ m1, q ^ m2, q]
        ps, qs = {
            "p1a_near": (p ^ 2, everything[:2]),
            "p1a_far": (p ^ 2, everything[2:]),
            "p1b_near": (p ^ m1, everything[:2]),
            "p1b_far": (p ^ m1, everything[2:]),
            "p2_near": (p ^ m2, everything[:2]),
            "p2_far": (p ^ m2, everything[2:]),
            "kept_near": (p, everything[:2]),
            "kept_far": (p, everything[2:]),
        }[which]
        offsets.append([block_offset(stream, ps, each, rows) for each in qs])
    return offsets


def gather(xt_ref, lhs, offsets, rows):
    for s in range(2):
        for b, offset in enumerate(offsets[s]):
            at = (s * len(offsets[s]) + b) * rows
            lhs[at : at + rows, :] = xt_ref[pl.ds(offset, rows), :]


def first_kernel(rows, tile, x_ref, dy_ref, xt_ref, dy_vmem, out0, out1, x_vmem, lhs, x_sems, dy_sems):
    x_rows = [pl.ds(at, tile) for at in range(0, x_ref.shape[0], tile)]
    dy_cols = [pl.ds(at, 2 * tile) for at in range(0, dy_ref.shape[1], 2 * tile)]
    x_copies = [pltpu.make_async_copy(x_ref.at[r, :], x_vmem.at[r, :], x_sems.at[t]) for t, r in enumerate(x_rows)]
    dy_copies = [pltpu.make_async_copy(dy_ref.at[:, c], dy_vmem.at[:, c], dy_sems.at[t]) for t, c in enumerate(dy_cols)]
    for copy in x_copies:
        copy.start()
    for t, (at, copy) in enumerate(zip(range(0, x_ref.shape[0], tile), x_copies)):
        copy.wait()
        if t == len(x_copies) // 2 - 1:
            dy_copies[0].start()
        if t == len(x_copies) - 1:
            for other in dy_copies[1:]:
                other.start()
        for cols in parts_of(x_ref, tile):
            xt_ref[cols, at : at + tile] = x_vmem[at : at + tile, cols].T
    gather(xt_ref, lhs, wanted("p1a_near", rows), rows)
    size = 2 * rows
    writers = [Writer(out0), Writer(out1)]
    for t, copy in enumerate(dy_copies):
        copy.wait()
        for cols in (slice(2 * t * tile, (2 * t + 1) * tile), slice((2 * t + 1) * tile, (2 * t + 2) * tile)):
            total = jnp.dot(lhs[...], dy_vmem[:, cols], preferred_element_type=F32)
            for s, put in enumerate(writers):
                put(total[s * size : (s + 1) * size])
    for put in writers:
        put.close()


def product_kernel(which, rows, tile, coded, pieces, xt_ref, dy_ref, *rest):
    arrivals, (_, _, out0, out1, lhs) = rest[:-5], rest[-5:]
    offsets = wanted(which, rows)
    size = len(offsets[0]) * rows
    gather(xt_ref, lhs, offsets, rows)
    readers = [Reader(ref, dy_ref.shape[1], rows) for ref in arrivals]
    writers = [Writer(out0), Writer(out1)]
    for cols in parts_of(dy_ref, tile):
        total = jnp.dot(lhs[...], dy_ref[:, cols], preferred_element_type=F32)
        for s, out in enumerate((out0, out1)):
            part = total[s * size : (s + 1) * size]
            if pieces:
                part += jnp.concatenate([readers[2 * k + s](at, count, cols) for k, at, count in pieces])
            if coded:
                writers[s](part)
            else:
                out[:, cols] = part
    if coded:
        for put in writers:
            put.close()


def params(mib):
    return pltpu.CompilerParams(vmem_limit_bytes=mib * 2**20)


def column(i):
    return (0, i)


VMEM = pl.BlockSpec(memory_space=pltpu.VMEM)


def product(which, rows, tile, xt, dy, arrivals, after, count=2, pieces=(), coded=True):
    tokens, cols = dy.shape
    size = count * rows
    shape = message(size, cols, False) if coded else jax.ShapeDtypeStruct((size, cols), F32)
    return pl.pallas_call(
        functools.partial(product_kernel, which, rows, tile, coded, pieces),
        out_shape=[shape, shape],
        in_specs=[VMEM] * (2 + len(arrivals)) + [pl.BlockSpec(memory_space=pl.ANY)] * 2,
        out_specs=[VMEM] * 2,
        scratch_shapes=[pltpu.VMEM((2 * size, tokens), BF16)],
        compiler_params=params(12),
        name=which,
    )(xt, dy, *arrivals, *after)


def first(rows, tile, x, dy):
    tokens, cols = dy.shape
    xt = jax.ShapeDtypeStruct((x.shape[1], tokens), BF16)
    return pl.pallas_call(
        functools.partial(first_kernel, rows, tile),
        out_shape=[xt, jax.ShapeDtypeStruct(dy.shape, BF16)] + [message(2 * rows, cols, False)] * 2,
        in_specs=[pl.BlockSpec(memory_space=pltpu.HBM)] * 2,
        out_specs=[VMEM] * 4,
        scratch_shapes=[
            pltpu.VMEM(x.shape, BF16),
            pltpu.VMEM((4 * rows, tokens), BF16),
            pltpu.SemaphoreType.DMA((tokens // tile,)),
            pltpu.SemaphoreType.DMA((cols // (2 * tile),)),
        ],
        compiler_params=params(40),
        name="p1a_near",
    )(x, dy)


def parts_of(ref, tile):
    for at in range(0, ref.shape[1], tile):
        yield slice(at, at + tile)


def near_kernel(rows, tile, kept0, kept1, arr0, arr1, *rest):
    for kept, arr, out in ((kept0, arr0, rest[-2]), (kept1, arr1, rest[-1])):
        read, put = Reader(arr, kept.shape[1], rows), Writer(out)
        for cols in parts_of(kept, tile):
            put(kept[:rows, cols] + read(0, 1, cols))
        put.close()


def far_kernel(rows, tile, kept0, kept1, arr0, arr1, *rest):
    for kept, arr, out in ((kept0, arr0, rest[-2]), (kept1, arr1, rest[-1])):
        read, put = Reader(arr, kept.shape[1], rows), Writer(out)
        for cols in parts_of(kept, tile):
            put(kept[rows:, cols] + read(1, 1, cols))
        put.close()


def add_kernel(rows, tile, kept0, kept1, arr0, arr1, out0, out1):
    for kept, arr, out in ((kept0, arr0, out0), (kept1, arr1, out1)):
        read = Reader(arr, kept.shape[1], rows)
        for cols in parts_of(kept, tile):
            out[:, cols] = kept[:, cols] + read(0, 2, cols)


def own_kernel(rows, tile, kept0, kept1, arr0, arr1, out):
    for s, (kept, arr) in enumerate(((kept0, arr0), (kept1, arr1))):
        read = Reader(arr, kept.shape[1], rows)
        for cols in parts_of(kept, tile):
            out[s * rows : (s + 1) * rows, cols] = kept[rows:, cols] + read(0, 1, cols)


def merge(name, kernel, rows, tile, ins, outs, after=()):
    return pl.pallas_call(
        functools.partial(kernel, rows, tile),
        out_shape=outs,
        in_specs=[VMEM] * len(ins) + [pl.BlockSpec(memory_space=pl.ANY)] * len(after),
        out_specs=[VMEM] * len(outs),
        compiler_params=params(12),
        name=name,
    )(*ins, *after)


def last_kernel(rows, far, own, arr0, arr1, *rest):
    _, y, _, core = coordinates()
    m1, m2 = masks(core)
    tiles = own.shape[1] // SIDE // LANES
    targets, outs = ((y ^ 2,), rest) if far else ((y ^ m1, y ^ m2, y), rest[1:])
    readers = [Reader(a, own.shape[1], rows) for a in (arr0, arr1)]
    for out, at in zip(outs, targets):
        put = Writer(out)
        for t in range(tiles):
            tile = at * tiles + t
            added = jnp.concatenate([read.dynamic(tile) for read in readers])
            put(own[:, pl.ds(pl.multiple_of(tile * LANES, LANES), LANES)] + added)
        put.close()


def last(rows, own, arrivals, after=()):
    count = 3 if after else 1
    return pl.pallas_call(
        functools.partial(last_kernel, rows, not after),
        out_shape=[message(2 * rows, own.shape[1] // SIDE, True)] * count,
        in_specs=[VMEM] * 3 + [pl.BlockSpec(memory_space=pl.ANY)] * len(after),
        out_specs=[VMEM] * count,
        compiler_params=params(12),
        name="last_near" if after else "last_far",
    )(own, *arrivals, *after)


def gram_kernel(rows, half, own0, own1, own2, own3, carr, g_ref, gram_ref):
    _, y, _, core = coordinates()
    m1, m2 = masks(core)
    wide = g_ref.shape[2]
    start = (wide - half) * core
    lane = lax.broadcasted_iota(jnp.int32, (1, wide), 1)
    valid = (lane >= start) & (lane < start + half)
    at = pl.ds(pl.multiple_of((own0.shape[1] - wide) * core, LANES), wide)
    sources = [(own0, 0, 0), (own1, m1, m2), (own2, m2, m1), (own3, 2, 2)]
    for k, (ref, mask, mask_other) in enumerate(sources):
        own = decode(ref[:rows, at], ref[rows : rows + 1, at].astype(F32))
        g_ref[(y ^ mask) * 2 + core] = jnp.where(valid, own, 0.0)
        other = decode(carr[k, :rows, :], carr[k, rows : rows + 1, :].astype(F32))
        g_ref[(y ^ mask_other) * 2 + 1 - core] = jnp.where(valid, other, 0.0)
    nodes = g_ref.shape[0]
    pairs = [(i, j) for i in range(nodes) for j in range(i, nodes)]

    def body(r, sums):
        blocks = [g_ref[n, pl.ds(r * 8, 8), :] for n in range(nodes)]
        out = []
        for total, (i, j) in zip(sums, pairs):
            product = blocks[i] * blocks[j]
            for t in range(wide // 128):
                total = total + product[:, t * 128 : (t + 1) * 128]
            out.append(total)
        return tuple(out)

    sums = lax.fori_loop(0, rows // 8, body, tuple(jnp.zeros((8, 128), F32) for _ in pairs))
    filled = [jnp.sum(total, axis=0, keepdims=True) for total in sums]
    filled += [jnp.zeros((1, 128), F32)] * (-len(pairs) % 8)
    stacked = jnp.sum(jnp.concatenate(filled), axis=1, keepdims=True)
    shape = (len(filled), 128)
    on = lax.broadcasted_iota(jnp.int32, shape, 0) == lax.broadcasted_iota(jnp.int32, shape, 1)
    row = jnp.sum(jnp.where(on, jnp.broadcast_to(stacked, shape), 0.0), axis=0, keepdims=True)
    gram_ref[...] = jnp.broadcast_to(row, gram_ref.shape)


def combine_kernel(half, g_ref, sums_ref, out_ref):
    nodes, rows, wide = g_ref.shape
    sums = jnp.sum(sums_ref[...], axis=0, keepdims=True)
    pairs = [(i, j) for i in range(nodes) for j in range(i, nodes)]
    gram = {}
    for k, (i, j) in enumerate(pairs):
        gram[i, j] = gram[j, i] = sums[:, k : k + 1]

    def inner(u, v):
        total = None
        for i, a in u.items():
            row = None
            for j, b in v.items():
                term = gram[i, j] * b
                row = term if row is None else row + term
            total = a * row if total is None else total + a * row
        return total

    one = jnp.ones((1, 1), F32)
    vectors = [{n: one} for n in range(nodes)]
    while len(vectors) > 1:
        middle = len(vectors) // 2
        merged = []
        for u, v in zip(vectors[:middle], vectors[middle:]):
            dot = inner(u, v)
            cu = 1.0 - dot / (2.0 * (inner(u, u) + EPS))
            cv = 1.0 - dot / (2.0 * (inner(v, v) + EPS))
            merged.append({**{n: cu * a for n, a in u.items()}, **{n: cv * a for n, a in v.items()}})
        vectors = merged
    total = None
    for n, coefficient in vectors[0].items():
        term = coefficient * g_ref[n]
        total = term if total is None else total + term
    core = lax.rem(lax.axis_index("node"), 2)
    moved = pltpu.roll(total, half, 1)
    out_ref[...] = jnp.where(core == 0, total[:, :half], moved[:, :half])


def local(x, dy):
    cols = dy.shape[1]
    rows = x.shape[1] // (2 * SIDE * SIDE)
    half = cols // (2 * SIDE)
    wide = -(-half // 128) * 128
    axes = ("x", "z")
    core = coordinates()[3]

    def send(pair, primary, is_first):
        return [exchange(m, axes[s] if primary else axes[1 - s], is_first) for s, m in enumerate(pair)]

    make = functools.partial(product, rows=rows, tile=256)
    xt, dyv, *m1 = first(rows, 256, x, dy)
    p1a_near = send(m1, True, True)
    m2 = make("p1a_far", xt=xt, dy=dyv, arrivals=[], after=m1)
    p1a_far = send(m2, True, True)
    p1b_near = send(make("p1b_near", xt=xt, dy=dyv, arrivals=[], after=m2), True, True)
    whole = ((0, 0, 2),)
    p2_near = send(make("p2_near", xt=xt, dy=dyv, arrivals=p1a_near, after=p1a_near, pieces=whole), True, False)
    m5 = make("p1b_far", xt=xt, dy=dyv, arrivals=[], after=p1a_far)
    p1b_far = send(m5, True, True)
    p2_far = send(make("p2_far", xt=xt, dy=dyv, arrivals=p1a_far, after=m5, pieces=whole), True, False)
    kept_near = make("kept_near", xt=xt, dy=dyv, arrivals=p1b_near, after=p1b_near, pieces=whole, coded=False)
    kept_far = make("kept_far", xt=xt, dy=dyv, arrivals=p1b_far, after=p1b_far, pieces=whole, coded=False)
    one = [message(rows, cols, False)] * 2
    two = [jax.ShapeDtypeStruct((2 * rows, cols), F32)] * 2
    q1_near = send(merge("q1_near", near_kernel, rows, 256, [*kept_near, *p2_near], one), False, True)
    q1_far = send(merge("q1_far", far_kernel, rows, 256, [*kept_near, *p2_near], one, p1b_far), False, True)
    rest = merge("rest", add_kernel, rows, 256, [*kept_far, *p2_far], two)
    q2 = send(merge("q2", near_kernel, rows, 256, [*rest, *q1_near], one), False, False)
    own = merge("own", own_kernel, rows, 256, [*rest, *q1_far], two[:1])
    far = last(rows, own[0], q2)
    near1, near2, mine = last(rows, own[0], q2, far)
    far = far[0]
    far = lax.ppermute(far, "node", [(i, i ^ 4) for i in range(2 * SIDE)])
    near1 = exchange(near1, "y", True)
    near2 = exchange(near2, "y", False)
    blocks = [mine, near1, near2, far]
    start = (cols // SIDE - wide) * (1 - core)
    across = jnp.stack([lax.dynamic_slice_in_dim(b, start, wide, axis=1) for b in blocks])
    carr = lax.ppermute(across, "node", [(i, i ^ 1) for i in range(2 * SIDE)])
    count = 2 * SIDE * SIDE * SIDE
    g, gram = pl.pallas_call(
        functools.partial(gram_kernel, 2 * rows, half),
        out_shape=[
            jax.ShapeDtypeStruct((2 * SIDE, 2 * rows, wide), F32),
            jax.ShapeDtypeStruct((count, 128), F32),
        ],
        compiler_params=params(12),
        name="gram",
    )(*blocks, carr)
    sums = lax.all_to_all(gram, ("node", "fsdp"), 0, 0, tiled=True)
    return pl.pallas_call(
        functools.partial(combine_kernel, half),
        out_shape=jax.ShapeDtypeStruct((2 * rows, half), F32),
        compiler_params=params(12),
        name="combine",
    )(g, sums)


def solution(mesh):
    in_specs = (P(("node", "fsdp"), None), P(("node", "fsdp"), None))
    out_specs = P("fsdp", "node")
    return jax.shard_map(local, mesh=mesh, in_specs=in_specs, out_specs=out_specs, check_vma=False)
```

```python
import functools

import jax
import jax.numpy as jnp
from jax import lax
from jax.experimental import pallas as pl
from jax.experimental.pallas import tpu as pltpu
from jax.sharding import PartitionSpec as P

EPS = 1e-06
POWER = 17
TOP = 2.0 ** (124 / POWER)
TINY = 2.0**-126
LANES = 128
WIDE_ROWS = 8
GROUP = 16
SIDE = 4
BF16, F32 = jnp.bfloat16, jnp.float32


def encode(values):
    peak = jnp.max(jnp.abs(values), axis=0, keepdims=True).astype(BF16).astype(F32)
    x = values * (TOP / jnp.maximum(peak, TINY))
    x2 = x * x
    x4 = x2 * x2
    x8 = x4 * x4
    return (x8 * x8 * x).astype(BF16), peak


def decode(code, peak):
    code = code.astype(F32)
    size = jnp.exp(jnp.log(jnp.abs(code)) * (1.0 / POWER))
    return jnp.where(code < 0, -size, size) * (peak * (1.0 / TOP))


def scale_rows(tiles):
    return -(-tiles // GROUP) * GROUP


def message(rows, cols, wide=False):
    tiles = cols // LANES
    if wide:
        return jax.ShapeDtypeStruct((rows + WIDE_ROWS, cols), BF16)
    return jax.ShapeDtypeStruct((tiles * rows + scale_rows(tiles), LANES), BF16)


class Reader:
    def __init__(self, ref, cols, rows):
        self.ref, self.rows = ref, rows
        tiles = cols // LANES
        self.wide = ref.shape[1] == cols
        if self.wide:
            self.height = ref.shape[0] - WIDE_ROWS
            return
        self.height = (ref.shape[0] - scale_rows(tiles)) // tiles
        self.scales = ref[tiles * self.height :, :].astype(F32)

    def __call__(self, at, count, cols):
        if self.wide:
            values = self.ref[at * self.rows : (at + count) * self.rows, cols]
            return decode(values, self.ref[self.height : self.height + 1, cols].astype(F32))
        out = []
        for t in range(cols.start // LANES, cols.stop // LANES):
            first = t * self.height + at * self.rows
            out.append(decode(self.ref[first : first + count * self.rows, :], self.scales[t : t + 1]))
        return jnp.concatenate(out, axis=1)

    def dynamic(self, tile):
        if self.wide:
            cols = pl.ds(pl.multiple_of(tile * LANES, LANES), LANES)
            return decode(self.ref[: self.height, cols], self.ref[self.height : self.height + 1, cols].astype(F32))
        on = lax.broadcasted_iota(jnp.int32, self.scales.shape, 0) == tile
        peak = jnp.sum(jnp.where(on, self.scales, 0.0), axis=0, keepdims=True)
        first = pl.multiple_of(tile * self.height, GROUP)
        return decode(self.ref[pl.ds(first, self.height), :], peak)


class Writer:
    def __init__(self, out):
        self.out, self.at, self.peaks = out, 0, []

    def __call__(self, values):
        code, peak = encode(values)
        rows, width = values.shape
        if self.out.shape[1] > LANES:
            cols = slice(self.at, self.at + width)
            self.out[:rows, cols] = code
            self.out[rows:, cols] = jnp.broadcast_to(peak, (WIDE_ROWS, width)).astype(BF16)
            self.at += width
            return
        for t in range(0, values.shape[1], LANES):
            self.out[self.at : self.at + rows, :] = code[:, t : t + LANES]
            self.at += rows
            self.peaks.append(peak[:, t : t + LANES])

    def close(self):
        if self.out.shape[1] > LANES:
            return
        spare = [jnp.zeros((1, LANES), F32)] * (scale_rows(len(self.peaks)) - len(self.peaks))
        self.out[self.at :, :] = jnp.concatenate(self.peaks + spare).astype(BF16)


def coordinates():
    node, fsdp = lax.axis_index("node"), lax.axis_index("fsdp")
    return lax.rem(fsdp, SIDE), node // 2, fsdp // SIDE, lax.rem(node, 2)


def masks(core):
    return 1 + 2 * core, 3 - 2 * core


def pairing(axis, first):
    pairs = []
    for y in range(SIDE):
        for core in range(2):
            mask = masks(core)[0 if first else 1]
            for z in range(SIDE):
                for x in range(SIDE):
                    at = dict(x=x, y=y, z=z)
                    to = dict(at)
                    to[axis] ^= mask
                    index = lambda p: (p["y"] * 2 + core) * SIDE * SIDE + p["z"] * SIDE + p["x"]
                    pairs.append((index(at), index(to)))
    return pairs


def exchange(array, axis, first):
    return lax.ppermute(array, ("node", "fsdp"), pairing(axis, first))


def block_offset(stream, p, q, rows):
    owner = jnp.where(stream == 0, q * SIDE + p, p * SIDE + q)
    return pl.multiple_of((owner * 2 + stream) * rows, 16)


def wanted(which, rows):
    x, _, z, core = coordinates()
    m1, m2 = masks(core)
    offsets = []
    for stream in range(2):
        p, q = (x, z) if stream == 0 else (z, x)
        everything = [q ^ 2, q ^ m1, q ^ m2, q]
        ps, qs = {
            "p1a_near": (p ^ 2, everything[:2]),
            "p1a_far": (p ^ 2, everything[2:]),
            "p1b_near": (p ^ m1, everything[:2]),
            "p1b_far": (p ^ m1, everything[2:]),
            "p2_near": (p ^ m2, everything[:2]),
            "p2_far": (p ^ m2, everything[2:]),
            "kept_near": (p, everything[:2]),
            "kept_far": (p, everything[2:]),
        }[which]
        offsets.append([block_offset(stream, ps, each, rows) for each in qs])
    return offsets


def gather(xt_ref, lhs, offsets, rows):
    for s in range(2):
        for b, offset in enumerate(offsets[s]):
            at = (s * len(offsets[s]) + b) * rows
            lhs[at : at + rows, :] = xt_ref[pl.ds(offset, rows), :]


def first_kernel(rows, tile, x_ref, dy_ref, xt_ref, dy_vmem, out0, out1, x_vmem, lhs, x_sems, dy_sems):
    x_rows = [pl.ds(at, tile) for at in range(0, x_ref.shape[0], tile)]
    dy_cols = [pl.ds(at, 2 * tile) for at in range(0, dy_ref.shape[1], 2 * tile)]
    x_copies = [pltpu.make_async_copy(x_ref.at[r, :], x_vmem.at[r, :], x_sems.at[t]) for t, r in enumerate(x_rows)]
    dy_copies = [pltpu.make_async_copy(dy_ref.at[:, c], dy_vmem.at[:, c], dy_sems.at[t]) for t, c in enumerate(dy_cols)]
    for copy in x_copies:
        copy.start()
    for t, (at, copy) in enumerate(zip(range(0, x_ref.shape[0], tile), x_copies)):
        copy.wait()
        if t == len(x_copies) // 2 - 1:
            dy_copies[0].start()
        if t == len(x_copies) - 1:
            for other in dy_copies[1:]:
                other.start()
        for cols in parts_of(x_ref, tile):
            xt_ref[cols, at : at + tile] = x_vmem[at : at + tile, cols].T
    gather(xt_ref, lhs, wanted("p1a_near", rows), rows)
    size = 2 * rows
    writers = [Writer(out0), Writer(out1)]
    for t, copy in enumerate(dy_copies):
        copy.wait()
        for cols in (slice(2 * t * tile, (2 * t + 1) * tile), slice((2 * t + 1) * tile, (2 * t + 2) * tile)):
            total = jnp.dot(lhs[...], dy_vmem[:, cols], preferred_element_type=F32)
            for s, put in enumerate(writers):
                put(total[s * size : (s + 1) * size])
    for put in writers:
        put.close()


def product_kernel(which, rows, tile, coded, pieces, xt_ref, dy_ref, *rest):
    arrivals, (_, _, out0, out1, lhs) = rest[:-5], rest[-5:]
    offsets = wanted(which, rows)
    size = len(offsets[0]) * rows
    gather(xt_ref, lhs, offsets, rows)
    readers = [Reader(ref, dy_ref.shape[1], rows) for ref in arrivals]
    writers = [Writer(out0), Writer(out1)]
    for cols in parts_of(dy_ref, tile):
        total = jnp.dot(lhs[...], dy_ref[:, cols], preferred_element_type=F32)
        for s, out in enumerate((out0, out1)):
            part = total[s * size : (s + 1) * size]
            if pieces:
                part += jnp.concatenate([readers[2 * k + s](at, count, cols) for k, at, count in pieces])
            if coded:
                writers[s](part)
            else:
                out[:, cols] = part
    if coded:
        for put in writers:
            put.close()


def params(mib):
    return pltpu.CompilerParams(vmem_limit_bytes=mib * 2**20)


def column(i):
    return (0, i)


VMEM = pl.BlockSpec(memory_space=pltpu.VMEM)


def product(which, rows, tile, xt, dy, arrivals, after, count=2, pieces=(), coded=True):
    tokens, cols = dy.shape
    size = count * rows
    shape = message(size, cols, False) if coded else jax.ShapeDtypeStruct((size, cols), F32)
    return pl.pallas_call(
        functools.partial(product_kernel, which, rows, tile, coded, pieces),
        out_shape=[shape, shape],
        in_specs=[VMEM] * (2 + len(arrivals)) + [pl.BlockSpec(memory_space=pl.ANY)] * 2,
        out_specs=[VMEM] * 2,
        scratch_shapes=[pltpu.VMEM((2 * size, tokens), BF16)],
        compiler_params=params(12),
        name=which,
    )(xt, dy, *arrivals, *after)


def first(rows, tile, x, dy):
    tokens, cols = dy.shape
    xt = jax.ShapeDtypeStruct((x.shape[1], tokens), BF16)
    return pl.pallas_call(
        functools.partial(first_kernel, rows, tile),
        out_shape=[xt, jax.ShapeDtypeStruct(dy.shape, BF16)] + [message(2 * rows, cols, False)] * 2,
        in_specs=[pl.BlockSpec(memory_space=pltpu.HBM)] * 2,
        out_specs=[VMEM] * 4,
        scratch_shapes=[
            pltpu.VMEM(x.shape, BF16),
            pltpu.VMEM((4 * rows, tokens), BF16),
            pltpu.SemaphoreType.DMA((tokens // tile,)),
            pltpu.SemaphoreType.DMA((cols // (2 * tile),)),
        ],
        compiler_params=params(40),
        name="p1a_near",
    )(x, dy)


def parts_of(ref, tile):
    for at in range(0, ref.shape[1], tile):
        yield slice(at, at + tile)


def near_kernel(rows, tile, kept0, kept1, arr0, arr1, *rest):
    for kept, arr, out in ((kept0, arr0, rest[-2]), (kept1, arr1, rest[-1])):
        read, put = Reader(arr, kept.shape[1], rows), Writer(out)
        for cols in parts_of(kept, tile):
            put(kept[:rows, cols] + read(0, 1, cols))
        put.close()


def far_kernel(rows, tile, kept0, kept1, arr0, arr1, *rest):
    for kept, arr, out in ((kept0, arr0, rest[-2]), (kept1, arr1, rest[-1])):
        read, put = Reader(arr, kept.shape[1], rows), Writer(out)
        for cols in parts_of(kept, tile):
            put(kept[rows:, cols] + read(1, 1, cols))
        put.close()


def q2_kernel(rows, tile, kept0, kept1, p0, p1, q0, q1, out0, out1):
    for kept, p, q, out in ((kept0, p0, q0, out0), (kept1, p1, q1, out1)):
        far, near, put = Reader(p, kept.shape[1], rows), Reader(q, kept.shape[1], rows), Writer(out)
        for cols in parts_of(kept, tile):
            put(kept[:rows, cols] + far(0, 1, cols) + near(0, 1, cols))
        put.close()


def own_kernel(rows, tile, kept0, kept1, p0, p1, q0, q1, out):
    for s, (kept, p, q) in enumerate(((kept0, p0, q0), (kept1, p1, q1))):
        far, near = Reader(p, kept.shape[1], rows), Reader(q, kept.shape[1], rows)
        for cols in parts_of(kept, tile):
            out[s * rows : (s + 1) * rows, cols] = kept[rows:, cols] + far(1, 1, cols) + near(0, 1, cols)


def merge(name, kernel, rows, tile, ins, outs, after=()):
    return pl.pallas_call(
        functools.partial(kernel, rows, tile),
        out_shape=outs,
        in_specs=[VMEM] * len(ins) + [pl.BlockSpec(memory_space=pl.ANY)] * len(after),
        out_specs=[VMEM] * len(outs),
        compiler_params=params(12),
        name=name,
    )(*ins, *after)


def last_kernel(rows, which, own, arr0, arr1, *rest):
    _, y, _, core = coordinates()
    m1, m2 = masks(core)
    tiles = own.shape[1] // SIDE // LANES
    targets = dict(far=(y ^ 2,), near=(y ^ m1, y ^ m2), mine=(y,))[which]
    outs = rest[-len(targets) :]
    readers = [Reader(a, own.shape[1], rows) for a in (arr0, arr1)]
    for out, at in zip(outs, targets):
        put = Writer(out)
        for t in range(tiles):
            tile = at * tiles + t
            added = jnp.concatenate([read.dynamic(tile) for read in readers])
            put(own[:, pl.ds(pl.multiple_of(tile * LANES, LANES), LANES)] + added)
        put.close()


def last(which, rows, own, arrivals, after=()):
    count = 2 if which == "near" else 1
    return pl.pallas_call(
        functools.partial(last_kernel, rows, which),
        out_shape=[message(2 * rows, own.shape[1] // SIDE, True)] * count,
        in_specs=[VMEM] * 3 + [pl.BlockSpec(memory_space=pl.ANY)] * len(after),
        out_specs=[VMEM] * count,
        compiler_params=params(12),
        name="last_" + which,
    )(own, *arrivals, *after)


def gram_kernel(rows, half, own0, own1, own2, own3, carr, g_ref, gram_ref):
    _, y, _, core = coordinates()
    m1, m2 = masks(core)
    wide = g_ref.shape[2]
    start = (wide - half) * core
    lane = lax.broadcasted_iota(jnp.int32, (1, wide), 1)
    valid = (lane >= start) & (lane < start + half)
    at = pl.ds(pl.multiple_of((own0.shape[1] - wide) * core, LANES), wide)
    sources = [(own0, 0, 0), (own1, m1, m2), (own2, m2, m1), (own3, 2, 2)]
    for k, (ref, mask, mask_other) in enumerate(sources):
        own = decode(ref[:rows, at], ref[rows : rows + 1, at].astype(F32))
        g_ref[(y ^ mask) * 2 + core] = jnp.where(valid, own, 0.0)
        other = decode(carr[k, :rows, :], carr[k, rows : rows + 1, :].astype(F32))
        g_ref[(y ^ mask_other) * 2 + 1 - core] = jnp.where(valid, other, 0.0)
    nodes = g_ref.shape[0]
    pairs = [(i, j) for i in range(nodes) for j in range(i, nodes)]

    def body(r, sums):
        blocks = [g_ref[n, pl.ds(r * 8, 8), :] for n in range(nodes)]
        out = []
        for total, (i, j) in zip(sums, pairs):
            product = blocks[i] * blocks[j]
            for t in range(wide // 128):
                total = total + product[:, t * 128 : (t + 1) * 128]
            out.append(total)
        return tuple(out)

    sums = lax.fori_loop(0, rows // 8, body, tuple(jnp.zeros((8, 128), F32) for _ in pairs))
    filled = [jnp.sum(total, axis=0, keepdims=True) for total in sums]
    filled += [jnp.zeros((1, 128), F32)] * (-len(pairs) % 8)
    stacked = jnp.sum(jnp.concatenate(filled), axis=1, keepdims=True)
    shape = (len(filled), 128)
    on = lax.broadcasted_iota(jnp.int32, shape, 0) == lax.broadcasted_iota(jnp.int32, shape, 1)
    row = jnp.sum(jnp.where(on, jnp.broadcast_to(stacked, shape), 0.0), axis=0, keepdims=True)
    gram_ref[...] = jnp.broadcast_to(row, gram_ref.shape)


def combine_kernel(half, g_ref, sums_ref, out_ref):
    nodes, rows, wide = g_ref.shape
    sums = jnp.sum(sums_ref[...], axis=0, keepdims=True)
    pairs = [(i, j) for i in range(nodes) for j in range(i, nodes)]
    gram = {}
    for k, (i, j) in enumerate(pairs):
        gram[i, j] = gram[j, i] = sums[:, k : k + 1]

    def inner(u, v):
        total = None
        for i, a in u.items():
            row = None
            for j, b in v.items():
                term = gram[i, j] * b
                row = term if row is None else row + term
            total = a * row if total is None else total + a * row
        return total

    one = jnp.ones((1, 1), F32)
    vectors = [{n: one} for n in range(nodes)]
    while len(vectors) > 1:
        middle = len(vectors) // 2
        merged = []
        for u, v in zip(vectors[:middle], vectors[middle:]):
            dot = inner(u, v)
            cu = 1.0 - dot / (2.0 * (inner(u, u) + EPS))
            cv = 1.0 - dot / (2.0 * (inner(v, v) + EPS))
            merged.append({**{n: cu * a for n, a in u.items()}, **{n: cv * a for n, a in v.items()}})
        vectors = merged
    total = None
    for n, coefficient in vectors[0].items():
        term = coefficient * g_ref[n]
        total = term if total is None else total + term
    core = lax.rem(lax.axis_index("node"), 2)
    moved = pltpu.roll(total, half, 1)
    out_ref[...] = jnp.where(core == 0, total[:, :half], moved[:, :half])


def local(x, dy):
    cols = dy.shape[1]
    rows = x.shape[1] // (2 * SIDE * SIDE)
    half = cols // (2 * SIDE)
    wide = -(-half // 128) * 128
    axes = ("x", "z")
    core = coordinates()[3]

    def send(pair, primary, is_first):
        return [exchange(m, axes[s] if primary else axes[1 - s], is_first) for s, m in enumerate(pair)]

    make = functools.partial(product, rows=rows, tile=256)
    xt, dyv, *m1 = first(rows, 256, x, dy)
    p1a_near = send(m1, True, True)
    m2 = make("p1a_far", xt=xt, dy=dyv, arrivals=[], after=m1)
    p1a_far = send(m2, True, True)
    p1b_near = send(make("p1b_near", xt=xt, dy=dyv, arrivals=[], after=m2), True, True)
    whole = ((0, 0, 2),)
    p2_near = send(make("p2_near", xt=xt, dy=dyv, arrivals=p1a_near, after=p1a_near, pieces=whole), True, False)
    m5 = make("p1b_far", xt=xt, dy=dyv, arrivals=[], after=p1a_far)
    p1b_far = send(m5, True, True)
    p2_far = send(make("p2_far", xt=xt, dy=dyv, arrivals=p1a_far, after=m5, pieces=whole), True, False)
    kept_near = make("kept_near", xt=xt, dy=dyv, arrivals=p1b_near, after=p1b_near, pieces=whole, coded=False)
    kept_far = make("kept_far", xt=xt, dy=dyv, arrivals=p1b_far, after=p1b_far, pieces=whole, coded=False)
    one = [message(rows, cols, False)] * 2
    q1_near = send(merge("q1_near", near_kernel, rows, 256, [*kept_near, *p2_near], one), False, True)
    q1_far = send(merge("q1_far", far_kernel, rows, 256, [*kept_near, *p2_near], one, p1b_far), False, True)
    q2 = send(merge("q2", q2_kernel, rows, 256, [*kept_far, *p2_far, *q1_near], one), False, False)
    own = merge("own", own_kernel, rows, 256, [*kept_far, *p2_far, *q1_far], [jax.ShapeDtypeStruct((2 * rows, cols), F32)])
    far = last("far", rows, own[0], q2)
    near = last("near", rows, own[0], q2, far)
    mine = last("mine", rows, own[0], q2, near)[0]
    far, (near1, near2) = far[0], near
    far = lax.ppermute(far, "node", [(i, i ^ 4) for i in range(2 * SIDE)])
    near1 = exchange(near1, "y", True)
    near2 = exchange(near2, "y", False)
    blocks = [mine, near1, near2, far]
    start = (cols // SIDE - wide) * (1 - core)
    across = jnp.stack([lax.dynamic_slice_in_dim(b, start, wide, axis=1) for b in blocks])
    carr = lax.ppermute(across, "node", [(i, i ^ 1) for i in range(2 * SIDE)])
    count = 2 * SIDE * SIDE * SIDE
    g, gram = pl.pallas_call(
        functools.partial(gram_kernel, 2 * rows, half),
        out_shape=[
            jax.ShapeDtypeStruct((2 * SIDE, 2 * rows, wide), F32),
            jax.ShapeDtypeStruct((count, 128), F32),
        ],
        compiler_params=params(12),
        name="gram",
    )(*blocks, carr)
    sums = lax.all_to_all(gram, ("node", "fsdp"), 0, 0, tiled=True)
    return pl.pallas_call(
        functools.partial(combine_kernel, half),
        out_shape=jax.ShapeDtypeStruct((2 * rows, half), F32),
        compiler_params=params(12),
        name="combine",
    )(g, sums)


def solution(mesh):
    in_specs = (P(("node", "fsdp"), None), P(("node", "fsdp"), None))
    out_specs = P("fsdp", "node")
    return jax.shard_map(local, mesh=mesh, in_specs=in_specs, out_specs=out_specs, check_vma=False)
```

```python
import functools

import jax
import jax.numpy as jnp
from jax import lax
from jax.experimental import pallas as pl
from jax.experimental.pallas import tpu as pltpu
from jax.sharding import PartitionSpec as P

EPS = 1e-06
POWER = 17
TOP = 2.0 ** (124 / POWER)
TINY = 2.0**-126
LANES = 128
WIDE_ROWS = 8
GROUP = 16
SIDE = 4
BF16, F32 = jnp.bfloat16, jnp.float32


def encode(values):
    peak = jnp.max(jnp.abs(values), axis=0, keepdims=True).astype(BF16).astype(F32)
    x = values * (TOP / jnp.maximum(peak, TINY))
    x2 = x * x
    x4 = x2 * x2
    x8 = x4 * x4
    return (x8 * x8 * x).astype(BF16), peak


def decode(code, peak):
    code = code.astype(F32)
    size = jnp.exp(jnp.log(jnp.abs(code)) * (1.0 / POWER))
    return jnp.where(code < 0, -size, size) * (peak * (1.0 / TOP))


def scale_rows(tiles):
    return -(-tiles // GROUP) * GROUP


def message(rows, cols, wide=False):
    tiles = cols // LANES
    if wide:
        return jax.ShapeDtypeStruct((rows + WIDE_ROWS, cols), BF16)
    return jax.ShapeDtypeStruct((tiles * rows + scale_rows(tiles), LANES), BF16)


class Reader:
    def __init__(self, ref, cols, rows):
        self.ref, self.rows = ref, rows
        tiles = cols // LANES
        self.wide = ref.shape[1] == cols
        if self.wide:
            self.height = ref.shape[0] - WIDE_ROWS
            return
        self.height = (ref.shape[0] - scale_rows(tiles)) // tiles
        self.scales = ref[tiles * self.height :, :].astype(F32)

    def __call__(self, at, count, cols):
        if self.wide:
            values = self.ref[at * self.rows : (at + count) * self.rows, cols]
            return decode(values, self.ref[self.height : self.height + 1, cols].astype(F32))
        out = []
        for t in range(cols.start // LANES, cols.stop // LANES):
            first = t * self.height + at * self.rows
            out.append(decode(self.ref[first : first + count * self.rows, :], self.scales[t : t + 1]))
        return jnp.concatenate(out, axis=1)

    def dynamic(self, tile):
        if self.wide:
            cols = pl.ds(pl.multiple_of(tile * LANES, LANES), LANES)
            return decode(self.ref[: self.height, cols], self.ref[self.height : self.height + 1, cols].astype(F32))
        on = lax.broadcasted_iota(jnp.int32, self.scales.shape, 0) == tile
        peak = jnp.sum(jnp.where(on, self.scales, 0.0), axis=0, keepdims=True)
        first = pl.multiple_of(tile * self.height, GROUP)
        return decode(self.ref[pl.ds(first, self.height), :], peak)


class Writer:
    def __init__(self, out):
        self.out, self.at, self.peaks = out, 0, []

    def __call__(self, values):
        code, peak = encode(values)
        rows, width = values.shape
        if self.out.shape[1] > LANES:
            cols = slice(self.at, self.at + width)
            self.out[:rows, cols] = code
            self.out[rows:, cols] = jnp.broadcast_to(peak, (WIDE_ROWS, width)).astype(BF16)
            self.at += width
            return
        for t in range(0, values.shape[1], LANES):
            self.out[self.at : self.at + rows, :] = code[:, t : t + LANES]
            self.at += rows
            self.peaks.append(peak[:, t : t + LANES])

    def close(self):
        if self.out.shape[1] > LANES:
            return
        spare = [jnp.zeros((1, LANES), F32)] * (scale_rows(len(self.peaks)) - len(self.peaks))
        self.out[self.at :, :] = jnp.concatenate(self.peaks + spare).astype(BF16)


def coordinates():
    node, fsdp = lax.axis_index("node"), lax.axis_index("fsdp")
    return lax.rem(fsdp, SIDE), node // 2, fsdp // SIDE, lax.rem(node, 2)


def masks(core):
    return 1 + 2 * core, 3 - 2 * core


def pairing(axis, first):
    pairs = []
    for y in range(SIDE):
        for core in range(2):
            mask = masks(core)[0 if first else 1]
            for z in range(SIDE):
                for x in range(SIDE):
                    at = dict(x=x, y=y, z=z)
                    to = dict(at)
                    to[axis] ^= mask
                    index = lambda p: (p["y"] * 2 + core) * SIDE * SIDE + p["z"] * SIDE + p["x"]
                    pairs.append((index(at), index(to)))
    return pairs


def exchange(array, axis, first):
    return lax.ppermute(array, ("node", "fsdp"), pairing(axis, first))


def block_offset(stream, p, q, rows):
    owner = jnp.where(stream == 0, q * SIDE + p, p * SIDE + q)
    return pl.multiple_of((owner * 2 + stream) * rows, 16)


def wanted(which, rows):
    x, _, z, core = coordinates()
    m1, m2 = masks(core)
    offsets = []
    for stream in range(2):
        p, q = (x, z) if stream == 0 else (z, x)
        everything = [q ^ 2, q ^ m1, q ^ m2, q]
        ps, qs = {
            "p1a_near": (p ^ 2, everything[:2]),
            "p1a_far": (p ^ 2, everything[2:]),
            "p1b_near": (p ^ m1, everything[:2]),
            "p1b_far": (p ^ m1, everything[2:]),
            "p2_near": (p ^ m2, everything[:2]),
            "p2_far": (p ^ m2, everything[2:]),
            "kept_near": (p, everything[:2]),
            "kept_far": (p, everything[2:]),
        }[which]
        offsets.append([block_offset(stream, ps, each, rows) for each in qs])
    return offsets


def gather(xt_ref, lhs, offsets, rows):
    for s in range(2):
        for b, offset in enumerate(offsets[s]):
            at = (s * len(offsets[s]) + b) * rows
            lhs[at : at + rows, :] = xt_ref[pl.ds(offset, rows), :]


def first_kernel(rows, tile, x_ref, dy_ref, xt_ref, dy_vmem, out0, out1, x_vmem, lhs, x_sems, dy_sems):
    x_rows = [pl.ds(at, tile) for at in range(0, x_ref.shape[0], tile)]
    dy_cols = [pl.ds(at, 2 * tile) for at in range(0, dy_ref.shape[1], 2 * tile)]
    x_copies = [pltpu.make_async_copy(x_ref.at[r, :], x_vmem.at[r, :], x_sems.at[t]) for t, r in enumerate(x_rows)]
    dy_copies = [pltpu.make_async_copy(dy_ref.at[:, c], dy_vmem.at[:, c], dy_sems.at[t]) for t, c in enumerate(dy_cols)]
    for copy in x_copies:
        copy.start()
    for t, (at, copy) in enumerate(zip(range(0, x_ref.shape[0], tile), x_copies)):
        copy.wait()
        if t == len(x_copies) // 2 - 1:
            dy_copies[0].start()
        if t == len(x_copies) - 1:
            for other in dy_copies[1:]:
                other.start()
        for cols in parts_of(x_ref, tile):
            xt_ref[cols, at : at + tile] = x_vmem[at : at + tile, cols].T
    gather(xt_ref, lhs, wanted("p1a_near", rows), rows)
    size = 2 * rows
    writers = [Writer(out0), Writer(out1)]
    for t, copy in enumerate(dy_copies):
        copy.wait()
        for cols in (slice(2 * t * tile, (2 * t + 1) * tile), slice((2 * t + 1) * tile, (2 * t + 2) * tile)):
            total = jnp.dot(lhs[...], dy_vmem[:, cols], preferred_element_type=F32)
            for s, put in enumerate(writers):
                put(total[s * size : (s + 1) * size])
    for put in writers:
        put.close()


def product_kernel(which, rows, tile, coded, pieces, xt_ref, dy_ref, *rest):
    arrivals, (_, _, out0, out1, lhs) = rest[:-5], rest[-5:]
    offsets = wanted(which, rows)
    size = len(offsets[0]) * rows
    gather(xt_ref, lhs, offsets, rows)
    readers = [Reader(ref, dy_ref.shape[1], rows) for ref in arrivals]
    writers = [Writer(out0), Writer(out1)]
    for cols in parts_of(dy_ref, tile):
        total = jnp.dot(lhs[...], dy_ref[:, cols], preferred_element_type=F32)
        for s, out in enumerate((out0, out1)):
            part = total[s * size : (s + 1) * size]
            if pieces:
                part += jnp.concatenate([readers[2 * k + s](at, count, cols) for k, at, count in pieces])
            if coded:
                writers[s](part)
            else:
                out[:, cols] = part
    if coded:
        for put in writers:
            put.close()


def params(mib):
    return pltpu.CompilerParams(vmem_limit_bytes=mib * 2**20)


def column(i):
    return (0, i)


VMEM = pl.BlockSpec(memory_space=pltpu.VMEM)


def product(which, rows, tile, xt, dy, arrivals, after, count=2, pieces=(), coded=True):
    tokens, cols = dy.shape
    size = count * rows
    shape = message(size, cols, False) if coded else jax.ShapeDtypeStruct((size, cols), F32)
    return pl.pallas_call(
        functools.partial(product_kernel, which, rows, tile, coded, pieces),
        out_shape=[shape, shape],
        in_specs=[VMEM] * (2 + len(arrivals)) + [pl.BlockSpec(memory_space=pl.ANY)] * 2,
        out_specs=[VMEM] * 2,
        scratch_shapes=[pltpu.VMEM((2 * size, tokens), BF16)],
        compiler_params=params(12),
        name=which,
    )(xt, dy, *arrivals, *after)


def first(rows, tile, x, dy):
    tokens, cols = dy.shape
    xt = jax.ShapeDtypeStruct((x.shape[1], tokens), BF16)
    return pl.pallas_call(
        functools.partial(first_kernel, rows, tile),
        out_shape=[xt, jax.ShapeDtypeStruct(dy.shape, BF16)] + [message(2 * rows, cols, False)] * 2,
        in_specs=[pl.BlockSpec(memory_space=pltpu.HBM)] * 2,
        out_specs=[VMEM] * 4,
        scratch_shapes=[
            pltpu.VMEM(x.shape, BF16),
            pltpu.VMEM((4 * rows, tokens), BF16),
            pltpu.SemaphoreType.DMA((tokens // tile,)),
            pltpu.SemaphoreType.DMA((cols // (2 * tile),)),
        ],
        compiler_params=params(40),
        name="p1a_near",
    )(x, dy)


def parts_of(ref, tile):
    for at in range(0, ref.shape[1], tile):
        yield slice(at, at + tile)


def near_kernel(rows, tile, kept0, kept1, arr0, arr1, *rest):
    for kept, arr, out in ((kept0, arr0, rest[-2]), (kept1, arr1, rest[-1])):
        read, put = Reader(arr, kept.shape[1], rows), Writer(out)
        for cols in parts_of(kept, tile):
            put(kept[:rows, cols] + read(0, 1, cols))
        put.close()


def far_kernel(rows, tile, kept0, kept1, arr0, arr1, *rest):
    for kept, arr, out in ((kept0, arr0, rest[-2]), (kept1, arr1, rest[-1])):
        read, put = Reader(arr, kept.shape[1], rows), Writer(out)
        for cols in parts_of(kept, tile):
            put(kept[rows:, cols] + read(1, 1, cols))
        put.close()


def targets(early):
    _, y, _, core = coordinates()
    m1, m2 = masks(core)
    return (y ^ 2, y ^ m1) if early else (y ^ m2, y)


def q2_kernel(rows, early, kept0, kept1, p0, p1, q0, q1, *rest):
    cols = kept0.shape[1]
    tiles = cols // SIDE // LANES
    for kept, p, q, out in ((kept0, p0, q0, rest[-2]), (kept1, p1, q1, rest[-1])):
        far, near, put = Reader(p, cols, rows), Reader(q, cols, rows), Writer(out)
        for target in targets(early):
            for t in range(tiles):
                tile = target * tiles + t
                at = pl.ds(pl.multiple_of(tile * LANES, LANES), LANES)
                put(kept[:rows, at] + far.dynamic(tile)[:rows] + near.dynamic(tile))
        put.close()


def own_kernel(rows, tile, kept0, kept1, p0, p1, q0, q1, out):
    for s, (kept, p, q) in enumerate(((kept0, p0, q0), (kept1, p1, q1))):
        far, near = Reader(p, kept.shape[1], rows), Reader(q, kept.shape[1], rows)
        for cols in parts_of(kept, tile):
            out[s * rows : (s + 1) * rows, cols] = kept[rows:, cols] + far(1, 1, cols) + near(0, 1, cols)


def merge(name, kernel, rows, tile, ins, outs, after=()):
    return pl.pallas_call(
        functools.partial(kernel, rows, tile),
        out_shape=outs,
        in_specs=[VMEM] * len(ins) + [pl.BlockSpec(memory_space=pl.ANY)] * len(after),
        out_specs=[VMEM] * len(outs),
        compiler_params=params(12),
        name=name,
    )(*ins, *after)


def last_kernel(rows, early, pick, own, arr0, arr1, *rest):
    tiles = own.shape[1] // SIDE // LANES
    readers = [Reader(a, own.shape[1] // 2, rows) for a in (arr0, arr1)]
    put = Writer(rest[-1])
    for t in range(tiles):
        at = (pick * tiles + t) * LANES
        added = jnp.concatenate([read(0, 1, slice(at, at + LANES)) for read in readers])
        tile = targets(early)[pick] * tiles + t
        put(own[:, pl.ds(pl.multiple_of(tile * LANES, LANES), LANES)] + added)
    put.close()


def last(name, rows, early, pick, own, arrivals, after=()):
    return pl.pallas_call(
        functools.partial(last_kernel, rows, early, pick),
        out_shape=[message(2 * rows, own.shape[1] // SIDE, True)],
        in_specs=[VMEM] * 3 + [pl.BlockSpec(memory_space=pl.ANY)] * len(after),
        out_specs=[VMEM],
        compiler_params=params(12),
        name=name,
    )(own, *arrivals, *after)


def cut_kernel(ref, *rest):
    out = rest[-1]
    wide = out.shape[1]
    at = pl.ds(pl.multiple_of((ref.shape[1] - wide) * (1 - coordinates()[3]), LANES), wide)
    out[...] = ref[:, at]


def gram_kernel(rows, half, own0, own1, own2, own3, carr, g_ref, gram_ref):
    _, y, _, core = coordinates()
    m1, m2 = masks(core)
    wide = g_ref.shape[2]
    start = (wide - half) * core
    lane = lax.broadcasted_iota(jnp.int32, (1, wide), 1)
    valid = (lane >= start) & (lane < start + half)
    at = pl.ds(pl.multiple_of((own0.shape[1] - wide) * core, LANES), wide)
    sources = [(own0, 0, 0), (own1, m1, m2), (own2, m2, m1), (own3, 2, 2)]
    for k, (ref, mask, mask_other) in enumerate(sources):
        own = decode(ref[:rows, at], ref[rows : rows + 1, at].astype(F32))
        g_ref[(y ^ mask) * 2 + core] = jnp.where(valid, own, 0.0)
        other = decode(carr[k, :rows, :], carr[k, rows : rows + 1, :].astype(F32))
        g_ref[(y ^ mask_other) * 2 + 1 - core] = jnp.where(valid, other, 0.0)
    nodes = g_ref.shape[0]
    pairs = [(i, j) for i in range(nodes) for j in range(i, nodes)]

    def body(r, sums):
        blocks = [g_ref[n, pl.ds(r * 8, 8), :] for n in range(nodes)]
        out = []
        for total, (i, j) in zip(sums, pairs):
            product = blocks[i] * blocks[j]
            for t in range(wide // 128):
                total = total + product[:, t * 128 : (t + 1) * 128]
            out.append(total)
        return tuple(out)

    sums = lax.fori_loop(0, rows // 8, body, tuple(jnp.zeros((8, 128), F32) for _ in pairs))
    filled = [jnp.sum(total, axis=0, keepdims=True) for total in sums]
    filled += [jnp.zeros((1, 128), F32)] * (-len(pairs) % 8)
    stacked = jnp.sum(jnp.concatenate(filled), axis=1, keepdims=True)
    shape = (len(filled), 128)
    on = lax.broadcasted_iota(jnp.int32, shape, 0) == lax.broadcasted_iota(jnp.int32, shape, 1)
    row = jnp.sum(jnp.where(on, jnp.broadcast_to(stacked, shape), 0.0), axis=0, keepdims=True)
    gram_ref[...] = jnp.broadcast_to(row, gram_ref.shape)


def combine_kernel(half, g_ref, sums_ref, out_ref):
    nodes, rows, wide = g_ref.shape
    sums = jnp.sum(sums_ref[...], axis=0, keepdims=True)
    pairs = [(i, j) for i in range(nodes) for j in range(i, nodes)]
    gram = {}
    for k, (i, j) in enumerate(pairs):
        gram[i, j] = gram[j, i] = sums[:, k : k + 1]

    def inner(u, v):
        total = None
        for i, a in u.items():
            row = None
            for j, b in v.items():
                term = gram[i, j] * b
                row = term if row is None else row + term
            total = a * row if total is None else total + a * row
        return total

    one = jnp.ones((1, 1), F32)
    vectors = [{n: one} for n in range(nodes)]
    while len(vectors) > 1:
        middle = len(vectors) // 2
        merged = []
        for u, v in zip(vectors[:middle], vectors[middle:]):
            dot = inner(u, v)
            cu = 1.0 - dot / (2.0 * (inner(u, u) + EPS))
            cv = 1.0 - dot / (2.0 * (inner(v, v) + EPS))
            merged.append({**{n: cu * a for n, a in u.items()}, **{n: cv * a for n, a in v.items()}})
        vectors = merged
    total = None
    for n, coefficient in vectors[0].items():
        term = coefficient * g_ref[n]
        total = term if total is None else total + term
    core = lax.rem(lax.axis_index("node"), 2)
    moved = pltpu.roll(total, half, 1)
    out_ref[...] = jnp.where(core == 0, total[:, :half], moved[:, :half])


def local(x, dy):
    cols = dy.shape[1]
    rows = x.shape[1] // (2 * SIDE * SIDE)
    half = cols // (2 * SIDE)
    wide = -(-half // 128) * 128
    axes = ("x", "z")
    core = coordinates()[3]

    def send(pair, primary, is_first):
        return [exchange(m, axes[s] if primary else axes[1 - s], is_first) for s, m in enumerate(pair)]

    make = functools.partial(product, rows=rows, tile=256)
    xt, dyv, *m1 = first(rows, 256, x, dy)
    p1a_near = send(m1, True, True)
    m2 = make("p1a_far", xt=xt, dy=dyv, arrivals=[], after=m1)
    p1a_far = send(m2, True, True)
    p1b_near = send(make("p1b_near", xt=xt, dy=dyv, arrivals=[], after=m2), True, True)
    whole = ((0, 0, 2),)
    p2_near = send(make("p2_near", xt=xt, dy=dyv, arrivals=p1a_near, after=p1a_near, pieces=whole), True, False)
    m5 = make("p1b_far", xt=xt, dy=dyv, arrivals=[], after=p1a_far)
    p1b_far = send(m5, True, True)
    p2_far = send(make("p2_far", xt=xt, dy=dyv, arrivals=p1a_far, after=m5, pieces=whole), True, False)
    kept_near = make("kept_near", xt=xt, dy=dyv, arrivals=p1b_near, after=p1b_near, pieces=whole, coded=False)
    kept_far = make("kept_far", xt=xt, dy=dyv, arrivals=p1b_far, after=p1b_far, pieces=whole, coded=False)
    one = [message(rows, cols, False)] * 2
    q1_near = send(merge("q1_near", near_kernel, rows, 256, [*kept_near, *p2_near], one), False, True)
    q1_far = send(merge("q1_far", far_kernel, rows, 256, [*kept_near, *p2_near], one, p1b_far), False, True)
    half_of = [message(rows, cols // 2)] * 2
    m9 = merge("q2_early", q2_kernel, rows, True, [*kept_far, *p2_far, *q1_near], half_of)
    q2_early = send(m9, False, False)
    q2_late = send(merge("q2_late", q2_kernel, rows, False, [*kept_far, *p2_far, *q1_near], half_of, m9), False, False)
    own = merge("own", own_kernel, rows, 256, [*kept_far, *p2_far, *q1_far], [jax.ShapeDtypeStruct((2 * rows, cols), F32)])[0]
    far = last("last_far", rows, True, 0, own, q2_early)
    near1 = last("last_near1", rows, True, 1, own, q2_early, far)
    near2 = last("last_near2", rows, False, 0, own, q2_late, near1)
    mine = last("last_mine", rows, False, 1, own, q2_late, near2)[0]
    far, near1, near2 = far[0], near1[0], near2[0]
    far = lax.ppermute(far, "node", [(i, i ^ 4) for i in range(2 * SIDE)])
    near1 = exchange(near1, "y", True)
    near2 = exchange(near2, "y", False)
    blocks = [mine, near1, near2, far]
    cuts, before = [], []
    for name, k in (("far", 3), ("near1", 1), ("near2", 2), ("mine", 0)):
        cut = pl.pallas_call(
            cut_kernel,
            out_shape=jax.ShapeDtypeStruct((blocks[0].shape[0], wide), BF16),
            in_specs=[VMEM] + [pl.BlockSpec(memory_space=pl.ANY)] * len(before),
            out_specs=VMEM,
            compiler_params=params(12),
            name="cut_" + name,
        )(blocks[k], *before)
        before = [cut] if name != "near2" else before
        cuts.append(cut)
    far_cut, near1_cut, near2_cut, mine_cut = cuts
    across = jnp.stack([mine_cut, near1_cut, near2_cut, far_cut])
    carr = lax.ppermute(across, "node", [(i, i ^ 1) for i in range(2 * SIDE)])
    count = 2 * SIDE * SIDE * SIDE
    g, gram = pl.pallas_call(
        functools.partial(gram_kernel, 2 * rows, half),
        out_shape=[
            jax.ShapeDtypeStruct((2 * SIDE, 2 * rows, wide), F32),
            jax.ShapeDtypeStruct((count, 128), F32),
        ],
        compiler_params=params(12),
        name="gram",
    )(*blocks, carr)
    sums = lax.all_to_all(gram, ("node", "fsdp"), 0, 0, tiled=True)
    return pl.pallas_call(
        functools.partial(combine_kernel, half),
        out_shape=jax.ShapeDtypeStruct((2 * rows, half), F32),
        compiler_params=params(12),
        name="combine",
    )(g, sums)


def solution(mesh):
    in_specs = (P(("node", "fsdp"), None), P(("node", "fsdp"), None))
    out_specs = P("fsdp", "node")
    return jax.shard_map(local, mesh=mesh, in_specs=in_specs, out_specs=out_specs, check_vma=False)
```

```python
import functools

import jax
import jax.numpy as jnp
from jax import lax
from jax.experimental import pallas as pl
from jax.experimental.pallas import tpu as pltpu
from jax.sharding import PartitionSpec as P

EPS = 1e-06
POWER = 17
TOP = 2.0 ** (124 / POWER)
TINY = 2.0**-118
LANES = 128
WIDE_ROWS = 8
GROUP = 16
SIDE = 4
BF16, F32 = jnp.bfloat16, jnp.float32


def encode(values):
    peak = jnp.maximum(jnp.max(jnp.abs(values), axis=0, keepdims=True), TINY).astype(BF16).astype(F32)
    x = values * (TOP / peak)
    x2 = x * x
    x4 = x2 * x2
    x8 = x4 * x4
    return (x8 * x8 * x).astype(BF16), peak


def decode(code, peak):
    code = code.astype(F32)
    size = jnp.exp(jnp.log(jnp.abs(code)) * (1.0 / POWER))
    return jnp.where(code < 0, -size, size) * (peak * (1.0 / TOP))


def scale_rows(tiles):
    return -(-tiles // GROUP) * GROUP


def message(rows, cols, wide=False):
    tiles = cols // LANES
    if wide:
        return jax.ShapeDtypeStruct((rows + WIDE_ROWS, cols), BF16)
    return jax.ShapeDtypeStruct((tiles * rows + scale_rows(tiles), LANES), BF16)


class Reader:
    def __init__(self, ref, cols, rows):
        self.ref, self.rows = ref, rows
        tiles = cols // LANES
        self.wide = ref.shape[1] == cols
        if self.wide:
            self.height = ref.shape[0] - WIDE_ROWS
            return
        self.height = (ref.shape[0] - scale_rows(tiles)) // tiles
        self.scales = ref[tiles * self.height :, :].astype(F32)

    def __call__(self, at, count, cols):
        if self.wide:
            values = self.ref[at * self.rows : (at + count) * self.rows, cols]
            return decode(values, self.ref[self.height : self.height + 1, cols].astype(F32))
        out = []
        for t in range(cols.start // LANES, cols.stop // LANES):
            first = t * self.height + at * self.rows
            out.append(decode(self.ref[first : first + count * self.rows, :], self.scales[t : t + 1]))
        return jnp.concatenate(out, axis=1)

    def dynamic(self, tile):
        if self.wide:
            cols = pl.ds(pl.multiple_of(tile * LANES, LANES), LANES)
            return decode(self.ref[: self.height, cols], self.ref[self.height : self.height + 1, cols].astype(F32))
        on = lax.broadcasted_iota(jnp.int32, self.scales.shape, 0) == tile
        peak = jnp.sum(jnp.where(on, self.scales, 0.0), axis=0, keepdims=True)
        first = pl.multiple_of(tile * self.height, GROUP)
        return decode(self.ref[pl.ds(first, self.height), :], peak)


class Writer:
    def __init__(self, out):
        self.out, self.at, self.peaks = out, 0, []

    def __call__(self, values):
        code, peak = encode(values)
        rows, width = values.shape
        if self.out.shape[1] > LANES:
            cols = slice(self.at, self.at + width)
            self.out[:rows, cols] = code
            self.out[rows:, cols] = jnp.broadcast_to(peak, (WIDE_ROWS, width)).astype(BF16)
            self.at += width
            return
        for t in range(0, values.shape[1], LANES):
            self.out[self.at : self.at + rows, :] = code[:, t : t + LANES]
            self.at += rows
            self.peaks.append(peak[:, t : t + LANES])

    def close(self):
        if self.out.shape[1] > LANES:
            return
        spare = [jnp.zeros((1, LANES), F32)] * (scale_rows(len(self.peaks)) - len(self.peaks))
        self.out[self.at :, :] = jnp.concatenate(self.peaks + spare).astype(BF16)


def coordinates():
    node, fsdp = lax.axis_index("node"), lax.axis_index("fsdp")
    return lax.rem(fsdp, SIDE), node // 2, fsdp // SIDE, lax.rem(node, 2)


def masks(core):
    return 1 + 2 * core, 3 - 2 * core


def pairing(axis, first):
    pairs = []
    for y in range(SIDE):
        for core in range(2):
            mask = masks(core)[0 if first else 1]
            for z in range(SIDE):
                for x in range(SIDE):
                    at = dict(x=x, y=y, z=z)
                    to = dict(at)
                    to[axis] ^= mask
                    index = lambda p: (p["y"] * 2 + core) * SIDE * SIDE + p["z"] * SIDE + p["x"]
                    pairs.append((index(at), index(to)))
    return pairs


def exchange(array, axis, first):
    return lax.ppermute(array, ("node", "fsdp"), pairing(axis, first))


def block_offset(stream, p, q, rows):
    owner = jnp.where(stream == 0, q * SIDE + p, p * SIDE + q)
    return pl.multiple_of((owner * 2 + stream) * rows, 16)


def wanted(which, rows):
    x, _, z, core = coordinates()
    m1, m2 = masks(core)
    offsets = []
    for stream in range(2):
        p, q = (x, z) if stream == 0 else (z, x)
        everything = [q ^ 2, q ^ m1, q ^ m2, q]
        ps, qs = {
            "p1a_near": (p ^ 2, everything[:2]),
            "p1a_far": (p ^ 2, everything[2:]),
            "p1b_near": (p ^ m1, everything[:2]),
            "p1b_far": (p ^ m1, everything[2:]),
            "p2_near": (p ^ m2, everything[:2]),
            "p2_far": (p ^ m2, everything[2:]),
            "kept_near": (p, everything[:2]),
            "kept_far": (p, everything[2:]),
        }[which]
        offsets.append([block_offset(stream, ps, each, rows) for each in qs])
    return offsets


def gather(xt_ref, lhs, offsets, rows):
    for s in range(2):
        for b, offset in enumerate(offsets[s]):
            at = (s * len(offsets[s]) + b) * rows
            lhs[at : at + rows, :] = xt_ref[pl.ds(offset, rows), :]


def first_kernel(rows, tile, x_ref, dy_ref, xt_ref, dy_vmem, out0, out1, x_vmem, lhs, x_sems, dy_sems):
    x_rows = [pl.ds(at, tile) for at in range(0, x_ref.shape[0], tile)]
    dy_cols = [pl.ds(at, 2 * tile) for at in range(0, dy_ref.shape[1], 2 * tile)]
    x_copies = [pltpu.make_async_copy(x_ref.at[r, :], x_vmem.at[r, :], x_sems.at[t]) for t, r in enumerate(x_rows)]
    dy_copies = [pltpu.make_async_copy(dy_ref.at[:, c], dy_vmem.at[:, c], dy_sems.at[t]) for t, c in enumerate(dy_cols)]
    for copy in x_copies:
        copy.start()
    for t, (at, copy) in enumerate(zip(range(0, x_ref.shape[0], tile), x_copies)):
        copy.wait()
        if t == len(x_copies) // 2 - 1:
            dy_copies[0].start()
        if t == len(x_copies) - 1:
            for other in dy_copies[1:]:
                other.start()
        for cols in parts_of(x_ref, tile):
            xt_ref[cols, at : at + tile] = x_vmem[at : at + tile, cols].T
    gather(xt_ref, lhs, wanted("p1a_near", rows), rows)
    size = 2 * rows
    writers = [Writer(out0), Writer(out1)]
    for t, copy in enumerate(dy_copies):
        copy.wait()
        for cols in (slice(2 * t * tile, (2 * t + 1) * tile), slice((2 * t + 1) * tile, (2 * t + 2) * tile)):
            total = jnp.dot(lhs[...], dy_vmem[:, cols], preferred_element_type=F32)
            for s, put in enumerate(writers):
                put(total[s * size : (s + 1) * size])
    for put in writers:
        put.close()


def product_kernel(which, rows, tile, coded, pieces, xt_ref, dy_ref, *rest):
    arrivals, (_, _, out0, out1, lhs) = rest[:-5], rest[-5:]
    offsets = wanted(which, rows)
    size = len(offsets[0]) * rows
    gather(xt_ref, lhs, offsets, rows)
    readers = [Reader(ref, dy_ref.shape[1], rows) for ref in arrivals]
    writers = [Writer(out0), Writer(out1)]
    for cols in parts_of(dy_ref, tile):
        total = jnp.dot(lhs[...], dy_ref[:, cols], preferred_element_type=F32)
        for s, out in enumerate((out0, out1)):
            part = total[s * size : (s + 1) * size]
            if pieces:
                part += jnp.concatenate([readers[2 * k + s](at, count, cols) for k, at, count in pieces])
            if coded:
                writers[s](part)
            else:
                out[:, cols] = part
    if coded:
        for put in writers:
            put.close()


def params(mib):
    return pltpu.CompilerParams(vmem_limit_bytes=mib * 2**20)


def column(i):
    return (0, i)


VMEM = pl.BlockSpec(memory_space=pltpu.VMEM)


def product(which, rows, tile, xt, dy, arrivals, after, count=2, pieces=(), coded=True):
    tokens, cols = dy.shape
    size = count * rows
    shape = message(size, cols, False) if coded else jax.ShapeDtypeStruct((size, cols), F32)
    return pl.pallas_call(
        functools.partial(product_kernel, which, rows, tile, coded, pieces),
        out_shape=[shape, shape],
        in_specs=[VMEM] * (2 + len(arrivals)) + [pl.BlockSpec(memory_space=pl.ANY)] * 2,
        out_specs=[VMEM] * 2,
        scratch_shapes=[pltpu.VMEM((2 * size, tokens), BF16)],
        compiler_params=params(12),
        name=which,
    )(xt, dy, *arrivals, *after)


def first(rows, tile, x, dy):
    tokens, cols = dy.shape
    xt = jax.ShapeDtypeStruct((x.shape[1], tokens), BF16)
    return pl.pallas_call(
        functools.partial(first_kernel, rows, tile),
        out_shape=[xt, jax.ShapeDtypeStruct(dy.shape, BF16)] + [message(2 * rows, cols, False)] * 2,
        in_specs=[pl.BlockSpec(memory_space=pltpu.HBM)] * 2,
        out_specs=[VMEM] * 4,
        scratch_shapes=[
            pltpu.VMEM(x.shape, BF16),
            pltpu.VMEM((4 * rows, tokens), BF16),
            pltpu.SemaphoreType.DMA((tokens // tile,)),
            pltpu.SemaphoreType.DMA((cols // (2 * tile),)),
        ],
        compiler_params=params(40),
        name="p1a_near",
    )(x, dy)


def parts_of(ref, tile):
    for at in range(0, ref.shape[1], tile):
        yield slice(at, at + tile)


def near_kernel(rows, tile, kept0, kept1, arr0, arr1, *rest):
    for kept, arr, out in ((kept0, arr0, rest[-2]), (kept1, arr1, rest[-1])):
        read, put = Reader(arr, kept.shape[1], rows), Writer(out)
        for cols in parts_of(kept, tile):
            put(kept[:rows, cols] + read(0, 1, cols))
        put.close()


def far_kernel(rows, tile, kept0, kept1, arr0, arr1, *rest):
    for kept, arr, out in ((kept0, arr0, rest[-2]), (kept1, arr1, rest[-1])):
        read, put = Reader(arr, kept.shape[1], rows), Writer(out)
        for cols in parts_of(kept, tile):
            put(kept[rows:, cols] + read(1, 1, cols))
        put.close()


def targets(early):
    _, y, _, core = coordinates()
    m1, m2 = masks(core)
    return (y ^ 2, y ^ m1) if early else (y ^ m2, y)


def q2_kernel(rows, early, kept0, kept1, p0, p1, q0, q1, *rest):
    cols = kept0.shape[1]
    tiles = cols // SIDE // LANES
    for kept, p, q, out in ((kept0, p0, q0, rest[-2]), (kept1, p1, q1, rest[-1])):
        far, near, put = Reader(p, cols, rows), Reader(q, cols, rows), Writer(out)
        for target in targets(early):
            for t in range(tiles):
                tile = target * tiles + t
                at = pl.ds(pl.multiple_of(tile * LANES, LANES), LANES)
                put(kept[:rows, at] + far.dynamic(tile)[:rows] + near.dynamic(tile))
        put.close()


def own_kernel(rows, tile, kept0, kept1, p0, p1, q0, q1, out):
    for s, (kept, p, q) in enumerate(((kept0, p0, q0), (kept1, p1, q1))):
        far, near = Reader(p, kept.shape[1], rows), Reader(q, kept.shape[1], rows)
        for cols in parts_of(kept, tile):
            out[s * rows : (s + 1) * rows, cols] = kept[rows:, cols] + far(1, 1, cols) + near(0, 1, cols)


def merge(name, kernel, rows, tile, ins, outs, after=()):
    return pl.pallas_call(
        functools.partial(kernel, rows, tile),
        out_shape=outs,
        in_specs=[VMEM] * len(ins) + [pl.BlockSpec(memory_space=pl.ANY)] * len(after),
        out_specs=[VMEM] * len(outs),
        compiler_params=params(12),
        name=name,
    )(*ins, *after)


def last_kernel(rows, early, pick, own, arr0, arr1, *rest):
    tiles = own.shape[1] // SIDE // LANES
    readers = [Reader(a, own.shape[1] // 2, rows) for a in (arr0, arr1)]
    put = Writer(rest[-1])
    for t in range(tiles):
        at = (pick * tiles + t) * LANES
        added = jnp.concatenate([read(0, 1, slice(at, at + LANES)) for read in readers])
        tile = targets(early)[pick] * tiles + t
        put(own[:, pl.ds(pl.multiple_of(tile * LANES, LANES), LANES)] + added)
    put.close()


def last(name, rows, early, pick, own, arrivals, after=()):
    return pl.pallas_call(
        functools.partial(last_kernel, rows, early, pick),
        out_shape=[message(2 * rows, own.shape[1] // SIDE, True)],
        in_specs=[VMEM] * 3 + [pl.BlockSpec(memory_space=pl.ANY)] * len(after),
        out_specs=[VMEM],
        compiler_params=params(12),
        name=name,
    )(own, *arrivals, *after)


def cut_kernel(ref, *rest):
    out = rest[-1]
    wide = out.shape[1]
    at = pl.ds(pl.multiple_of((ref.shape[1] - wide) * (1 - coordinates()[3]), LANES), wide)
    out[...] = ref[:, at]


def gram_kernel(rows, half, own0, own1, own2, own3, carr, g_ref, gram_ref):
    _, y, _, core = coordinates()
    m1, m2 = masks(core)
    wide = g_ref.shape[2]
    start = (wide - half) * core
    lane = lax.broadcasted_iota(jnp.int32, (1, wide), 1)
    valid = (lane >= start) & (lane < start + half)
    at = pl.ds(pl.multiple_of((own0.shape[1] - wide) * core, LANES), wide)
    sources = [(own0, 0, 0), (own1, m1, m2), (own2, m2, m1), (own3, 2, 2)]
    for k, (ref, mask, mask_other) in enumerate(sources):
        own = decode(ref[:rows, at], ref[rows : rows + 1, at].astype(F32))
        g_ref[(y ^ mask) * 2 + core] = jnp.where(valid, own, 0.0)
        other = decode(carr[k, :rows, :], carr[k, rows : rows + 1, :].astype(F32))
        g_ref[(y ^ mask_other) * 2 + 1 - core] = jnp.where(valid, other, 0.0)
    nodes = g_ref.shape[0]
    pairs = [(i, j) for i in range(nodes) for j in range(i, nodes)]

    def body(r, sums):
        blocks = [g_ref[n, pl.ds(r * 8, 8), :] for n in range(nodes)]
        out = []
        for total, (i, j) in zip(sums, pairs):
            product = blocks[i] * blocks[j]
            for t in range(wide // 128):
                total = total + product[:, t * 128 : (t + 1) * 128]
            out.append(total)
        return tuple(out)

    sums = lax.fori_loop(0, rows // 8, body, tuple(jnp.zeros((8, 128), F32) for _ in pairs))
    filled = [jnp.sum(total, axis=0, keepdims=True) for total in sums]
    filled += [jnp.zeros((1, 128), F32)] * (-len(pairs) % 8)
    stacked = jnp.sum(jnp.concatenate(filled), axis=1, keepdims=True)
    shape = (len(filled), 128)
    on = lax.broadcasted_iota(jnp.int32, shape, 0) == lax.broadcasted_iota(jnp.int32, shape, 1)
    row = jnp.sum(jnp.where(on, jnp.broadcast_to(stacked, shape), 0.0), axis=0, keepdims=True)
    gram_ref[...] = jnp.broadcast_to(row, gram_ref.shape)


def combine_kernel(half, g_ref, sums_ref, out_ref):
    nodes, rows, wide = g_ref.shape
    sums = jnp.sum(sums_ref[...], axis=0, keepdims=True)
    pairs = [(i, j) for i in range(nodes) for j in range(i, nodes)]
    gram = {}
    for k, (i, j) in enumerate(pairs):
        gram[i, j] = gram[j, i] = sums[:, k : k + 1]

    def inner(u, v):
        total = None
        for i, a in u.items():
            row = None
            for j, b in v.items():
                term = gram[i, j] * b
                row = term if row is None else row + term
            total = a * row if total is None else total + a * row
        return total

    one = jnp.ones((1, 1), F32)
    vectors = [{n: one} for n in range(nodes)]
    while len(vectors) > 1:
        middle = len(vectors) // 2
        merged = []
        for u, v in zip(vectors[:middle], vectors[middle:]):
            dot = inner(u, v)
            cu = 1.0 - dot / (2.0 * (inner(u, u) + EPS))
            cv = 1.0 - dot / (2.0 * (inner(v, v) + EPS))
            merged.append({**{n: cu * a for n, a in u.items()}, **{n: cv * a for n, a in v.items()}})
        vectors = merged
    total = None
    for n, coefficient in vectors[0].items():
        term = coefficient * g_ref[n]
        total = term if total is None else total + term
    core = lax.rem(lax.axis_index("node"), 2)
    moved = pltpu.roll(total, half, 1)
    out_ref[...] = jnp.where(core == 0, total[:, :half], moved[:, :half])


def local(x, dy):
    cols = dy.shape[1]
    rows = x.shape[1] // (2 * SIDE * SIDE)
    half = cols // (2 * SIDE)
    wide = -(-half // 128) * 128
    axes = ("x", "z")
    core = coordinates()[3]

    def send(pair, primary, is_first):
        return [exchange(m, axes[s] if primary else axes[1 - s], is_first) for s, m in enumerate(pair)]

    make = functools.partial(product, rows=rows, tile=256)
    xt, dyv, *m1 = first(rows, 256, x, dy)
    p1a_near = send(m1, True, True)
    m2 = make("p1a_far", xt=xt, dy=dyv, arrivals=[], after=m1)
    p1a_far = send(m2, True, True)
    p1b_near = send(make("p1b_near", xt=xt, dy=dyv, arrivals=[], after=m2), True, True)
    whole = ((0, 0, 2),)
    p2_near = send(make("p2_near", xt=xt, dy=dyv, arrivals=p1a_near, after=p1a_near, pieces=whole), True, False)
    m5 = make("p1b_far", xt=xt, dy=dyv, arrivals=[], after=p1a_far)
    p1b_far = send(m5, True, True)
    p2_far = send(make("p2_far", xt=xt, dy=dyv, arrivals=p1a_far, after=m5, pieces=whole), True, False)
    kept_near = make("kept_near", xt=xt, dy=dyv, arrivals=p1b_near, after=p1b_near, pieces=whole, coded=False)
    kept_far = make("kept_far", xt=xt, dy=dyv, arrivals=p1b_far, after=p1b_far, pieces=whole, coded=False)
    one = [message(rows, cols, False)] * 2
    q1_near = send(merge("q1_near", near_kernel, rows, 256, [*kept_near, *p2_near], one), False, True)
    q1_far = send(merge("q1_far", far_kernel, rows, 256, [*kept_near, *p2_near], one, p1b_far), False, True)
    half_of = [message(rows, cols // 2)] * 2
    m9 = merge("q2_early", q2_kernel, rows, True, [*kept_far, *p2_far, *q1_near], half_of)
    q2_early = send(m9, False, False)
    q2_late = send(merge("q2_late", q2_kernel, rows, False, [*kept_far, *p2_far, *q1_near], half_of, m9), False, False)
    own = merge("own", own_kernel, rows, 256, [*kept_far, *p2_far, *q1_far], [jax.ShapeDtypeStruct((2 * rows, cols), F32)])[0]
    far = last("last_far", rows, True, 0, own, q2_early)
    near1 = last("last_near1", rows, True, 1, own, q2_early, far)
    near2 = last("last_near2", rows, False, 0, own, q2_late, near1)
    mine = last("last_mine", rows, False, 1, own, q2_late, near2)[0]
    far, near1, near2 = far[0], near1[0], near2[0]
    far = lax.ppermute(far, "node", [(i, i ^ 4) for i in range(2 * SIDE)])
    near1 = exchange(near1, "y", True)
    near2 = exchange(near2, "y", False)
    blocks = [mine, near1, near2, far]
    cuts, before = [], []
    for name, k in (("far", 3), ("near1", 1), ("near2", 2), ("mine", 0)):
        cut = pl.pallas_call(
            cut_kernel,
            out_shape=jax.ShapeDtypeStruct((blocks[0].shape[0], wide), BF16),
            in_specs=[VMEM] + [pl.BlockSpec(memory_space=pl.ANY)] * len(before),
            out_specs=VMEM,
            compiler_params=params(12),
            name="cut_" + name,
        )(blocks[k], *before)
        before = [cut] if name != "near2" else before
        cuts.append(cut)
    far_cut, near1_cut, near2_cut, mine_cut = cuts
    across = jnp.stack([mine_cut, near1_cut, near2_cut, far_cut])
    carr = lax.ppermute(across, "node", [(i, i ^ 1) for i in range(2 * SIDE)])
    count = 2 * SIDE * SIDE * SIDE
    g, gram = pl.pallas_call(
        functools.partial(gram_kernel, 2 * rows, half),
        out_shape=[
            jax.ShapeDtypeStruct((2 * SIDE, 2 * rows, wide), F32),
            jax.ShapeDtypeStruct((count, 128), F32),
        ],
        compiler_params=params(12),
        name="gram",
    )(*blocks, carr)
    sums = lax.all_to_all(gram, ("node", "fsdp"), 0, 0, tiled=True)
    return pl.pallas_call(
        functools.partial(combine_kernel, half),
        out_shape=jax.ShapeDtypeStruct((2 * rows, half), F32),
        compiler_params=params(12),
        name="combine",
    )(g, sums)


def solution(mesh):
    in_specs = (P(("node", "fsdp"), None), P(("node", "fsdp"), None))
    out_specs = P("fsdp", "node")
    return jax.shard_map(local, mesh=mesh, in_specs=in_specs, out_specs=out_specs, check_vma=False)
```

```python
import functools

import jax
import jax.numpy as jnp
from jax import lax
from jax.experimental import pallas as pl
from jax.experimental.pallas import tpu as pltpu
from jax.sharding import PartitionSpec as P

EPS = 1e-06
POWER = 17
TOP = 2.0 ** (124 / POWER)
TINY = 2.0**-118
LANES = 128
WIDE_ROWS = 8
GROUP = 16
SIDE = 4
BF16, F32 = jnp.bfloat16, jnp.float32


def encode(values):
    peak = jnp.maximum(jnp.max(jnp.abs(values), axis=0, keepdims=True), TINY).astype(BF16).astype(F32)
    x = values * (TOP / peak)
    x2 = x * x
    x4 = x2 * x2
    x8 = x4 * x4
    return (x8 * x8 * x).astype(BF16), peak


def decode(code, peak):
    code = code.astype(F32)
    size = jnp.exp(jnp.log(jnp.abs(code)) * (1.0 / POWER))
    return jnp.where(code < 0, -size, size) * (peak * (1.0 / TOP))


def scale_rows(tiles):
    return -(-tiles // GROUP) * GROUP


def message(rows, cols, wide=False):
    tiles = cols // LANES
    if wide:
        return jax.ShapeDtypeStruct((rows + WIDE_ROWS, cols), BF16)
    return jax.ShapeDtypeStruct((tiles * rows + scale_rows(tiles), LANES), BF16)


class Reader:
    def __init__(self, ref, cols, rows):
        self.ref, self.rows = ref, rows
        tiles = cols // LANES
        self.wide = ref.shape[1] == cols
        if self.wide:
            self.height = ref.shape[0] - WIDE_ROWS
            return
        self.height = (ref.shape[0] - scale_rows(tiles)) // tiles
        self.scales = ref[tiles * self.height :, :].astype(F32)

    def __call__(self, at, count, cols):
        if self.wide:
            values = self.ref[at * self.rows : (at + count) * self.rows, cols]
            return decode(values, self.ref[self.height : self.height + 1, cols].astype(F32))
        out = []
        for t in range(cols.start // LANES, cols.stop // LANES):
            first = t * self.height + at * self.rows
            out.append(decode(self.ref[first : first + count * self.rows, :], self.scales[t : t + 1]))
        return jnp.concatenate(out, axis=1)

    def dynamic(self, tile):
        if self.wide:
            cols = pl.ds(pl.multiple_of(tile * LANES, LANES), LANES)
            return decode(self.ref[: self.height, cols], self.ref[self.height : self.height + 1, cols].astype(F32))
        on = lax.broadcasted_iota(jnp.int32, self.scales.shape, 0) == tile
        peak = jnp.sum(jnp.where(on, self.scales, 0.0), axis=0, keepdims=True)
        first = pl.multiple_of(tile * self.height, GROUP)
        return decode(self.ref[pl.ds(first, self.height), :], peak)


class Writer:
    def __init__(self, out):
        self.out, self.at, self.peaks = out, 0, []

    def __call__(self, values):
        code, peak = encode(values)
        rows, width = values.shape
        if self.out.shape[1] > LANES:
            cols = slice(self.at, self.at + width)
            self.out[:rows, cols] = code
            self.out[rows:, cols] = jnp.broadcast_to(peak, (WIDE_ROWS, width)).astype(BF16)
            self.at += width
            return
        for t in range(0, values.shape[1], LANES):
            self.out[self.at : self.at + rows, :] = code[:, t : t + LANES]
            self.at += rows
            self.peaks.append(peak[:, t : t + LANES])

    def close(self):
        if self.out.shape[1] > LANES:
            return
        spare = [jnp.zeros((1, LANES), F32)] * (scale_rows(len(self.peaks)) - len(self.peaks))
        self.out[self.at :, :] = jnp.concatenate(self.peaks + spare).astype(BF16)


def coordinates():
    node, fsdp = lax.axis_index("node"), lax.axis_index("fsdp")
    return lax.rem(fsdp, SIDE), node // 2, fsdp // SIDE, lax.rem(node, 2)


def masks(core):
    return 1 + 2 * core, 3 - 2 * core


def pairing(axis, first):
    pairs = []
    for y in range(SIDE):
        for core in range(2):
            mask = masks(core)[0 if first else 1]
            for z in range(SIDE):
                for x in range(SIDE):
                    at = dict(x=x, y=y, z=z)
                    to = dict(at)
                    to[axis] ^= mask
                    index = lambda p: (p["y"] * 2 + core) * SIDE * SIDE + p["z"] * SIDE + p["x"]
                    pairs.append((index(at), index(to)))
    return pairs


def exchange(array, axis, first):
    return lax.ppermute(array, ("node", "fsdp"), pairing(axis, first))


def block_offset(stream, p, q, rows):
    owner = jnp.where(stream == 0, q * SIDE + p, p * SIDE + q)
    return pl.multiple_of((owner * 2 + stream) * rows, 16)


def wanted(which, rows):
    x, _, z, core = coordinates()
    m1, m2 = masks(core)
    offsets = []
    for stream in range(2):
        p, q = (x, z) if stream == 0 else (z, x)
        everything = [q ^ 2, q ^ m1, q ^ m2, q]
        ps, qs = {
            "p1a_near": (p ^ 2, everything[:2]),
            "p1a_far": (p ^ 2, everything[2:]),
            "p1b_near": (p ^ m1, everything[:2]),
            "p1b_far": (p ^ m1, everything[2:]),
            "p2_near": (p ^ m2, everything[:2]),
            "p2_far": (p ^ m2, everything[2:]),
            "kept_near": (p, everything[:2]),
            "kept_far": (p, everything[2:]),
        }[which]
        offsets.append([block_offset(stream, ps, each, rows) for each in qs])
    return offsets


def gather(xt_ref, lhs, offsets, rows):
    for s in range(2):
        for b, offset in enumerate(offsets[s]):
            at = (s * len(offsets[s]) + b) * rows
            lhs[at : at + rows, :] = xt_ref[pl.ds(offset, rows), :]


def first_kernel(rows, tile, x_ref, dy_ref, xt_ref, dy_vmem, out0, out1, x_vmem, lhs, x_sems, dy_sems):
    x_rows = [pl.ds(at, tile) for at in range(0, x_ref.shape[0], tile)]
    dy_cols = [pl.ds(at, 2 * tile) for at in range(0, dy_ref.shape[1], 2 * tile)]
    x_copies = [pltpu.make_async_copy(x_ref.at[r, :], x_vmem.at[r, :], x_sems.at[t]) for t, r in enumerate(x_rows)]
    dy_copies = [pltpu.make_async_copy(dy_ref.at[:, c], dy_vmem.at[:, c], dy_sems.at[t]) for t, c in enumerate(dy_cols)]
    for copy in x_copies:
        copy.start()
    for t, (at, copy) in enumerate(zip(range(0, x_ref.shape[0], tile), x_copies)):
        copy.wait()
        if t == len(x_copies) // 2 - 1:
            dy_copies[0].start()
        if t == len(x_copies) - 1:
            for other in dy_copies[1:]:
                other.start()
        for cols in parts_of(x_ref, tile):
            xt_ref[cols, at : at + tile] = x_vmem[at : at + tile, cols].T
    gather(xt_ref, lhs, wanted("p1a_near", rows), rows)
    size = 2 * rows
    writers = [Writer(out0), Writer(out1)]
    for t, copy in enumerate(dy_copies):
        copy.wait()
        for cols in (slice(2 * t * tile, (2 * t + 1) * tile), slice((2 * t + 1) * tile, (2 * t + 2) * tile)):
            total = jnp.dot(lhs[...], dy_vmem[:, cols], preferred_element_type=F32)
            for s, put in enumerate(writers):
                put(total[s * size : (s + 1) * size])
    for put in writers:
        put.close()


def product_kernel(which, rows, tile, coded, pieces, xt_ref, dy_ref, *rest):
    arrivals, (_, _, out0, out1, lhs) = rest[:-5], rest[-5:]
    offsets = wanted(which, rows)
    size = len(offsets[0]) * rows
    gather(xt_ref, lhs, offsets, rows)
    readers = [Reader(ref, dy_ref.shape[1], rows) for ref in arrivals]
    writers = [Writer(out0), Writer(out1)]
    for cols in parts_of(dy_ref, tile):
        total = jnp.dot(lhs[...], dy_ref[:, cols], preferred_element_type=F32)
        for s, out in enumerate((out0, out1)):
            part = total[s * size : (s + 1) * size]
            if pieces:
                part += jnp.concatenate([readers[2 * k + s](at, count, cols) for k, at, count in pieces])
            if coded:
                writers[s](part)
            else:
                out[:, cols] = part
    if coded:
        for put in writers:
            put.close()


def params(mib):
    return pltpu.CompilerParams(vmem_limit_bytes=mib * 2**20)


def column(i):
    return (0, i)


VMEM = pl.BlockSpec(memory_space=pltpu.VMEM)


def product(which, rows, tile, xt, dy, arrivals, after, count=2, pieces=(), coded=True):
    tokens, cols = dy.shape
    size = count * rows
    shape = message(size, cols, False) if coded else jax.ShapeDtypeStruct((size, cols), F32)
    return pl.pallas_call(
        functools.partial(product_kernel, which, rows, tile, coded, pieces),
        out_shape=[shape, shape],
        in_specs=[VMEM] * (2 + len(arrivals)) + [pl.BlockSpec(memory_space=pl.ANY)] * 2,
        out_specs=[VMEM] * 2,
        scratch_shapes=[pltpu.VMEM((2 * size, tokens), BF16)],
        compiler_params=params(12),
        name=which,
    )(xt, dy, *arrivals, *after)


def first(rows, tile, x, dy):
    tokens, cols = dy.shape
    xt = jax.ShapeDtypeStruct((x.shape[1], tokens), BF16)
    return pl.pallas_call(
        functools.partial(first_kernel, rows, tile),
        out_shape=[xt, jax.ShapeDtypeStruct(dy.shape, BF16)] + [message(2 * rows, cols, False)] * 2,
        in_specs=[pl.BlockSpec(memory_space=pltpu.HBM)] * 2,
        out_specs=[VMEM] * 4,
        scratch_shapes=[
            pltpu.VMEM(x.shape, BF16),
            pltpu.VMEM((4 * rows, tokens), BF16),
            pltpu.SemaphoreType.DMA((tokens // tile,)),
            pltpu.SemaphoreType.DMA((cols // (2 * tile),)),
        ],
        compiler_params=params(40),
        name="p1a_near",
    )(x, dy)


def parts_of(ref, tile):
    for at in range(0, ref.shape[1], tile):
        yield slice(at, at + tile)


def near_kernel(rows, tile, kept0, kept1, arr0, arr1, *rest):
    for kept, arr, out in ((kept0, arr0, rest[-2]), (kept1, arr1, rest[-1])):
        read, put = Reader(arr, kept.shape[1], rows), Writer(out)
        for cols in parts_of(kept, tile):
            put(kept[:rows, cols] + read(0, 1, cols))
        put.close()


def far_kernel(rows, tile, kept0, kept1, arr0, arr1, *rest):
    for kept, arr, out in ((kept0, arr0, rest[-2]), (kept1, arr1, rest[-1])):
        read, put = Reader(arr, kept.shape[1], rows), Writer(out)
        for cols in parts_of(kept, tile):
            put(kept[rows:, cols] + read(1, 1, cols))
        put.close()


def targets(early):
    _, y, _, core = coordinates()
    m1, m2 = masks(core)
    return (y ^ 2, y ^ m1) if early else (y ^ m2, y)


def q2_kernel(rows, early, kept0, kept1, p0, p1, q0, q1, *rest):
    cols = kept0.shape[1]
    tiles = cols // SIDE // LANES
    for kept, p, q, out in ((kept0, p0, q0, rest[-2]), (kept1, p1, q1, rest[-1])):
        far, near, put = Reader(p, cols, rows), Reader(q, cols, rows), Writer(out)
        for target in targets(early):
            for t in range(tiles):
                tile = target * tiles + t
                at = pl.ds(pl.multiple_of(tile * LANES, LANES), LANES)
                put(kept[:rows, at] + far.dynamic(tile)[:rows] + near.dynamic(tile))
        put.close()


def own_kernel(rows, tile, kept0, kept1, p0, p1, q0, q1, out):
    for s, (kept, p, q) in enumerate(((kept0, p0, q0), (kept1, p1, q1))):
        far, near = Reader(p, kept.shape[1], rows), Reader(q, kept.shape[1], rows)
        for cols in parts_of(kept, tile):
            out[s * rows : (s + 1) * rows, cols] = kept[rows:, cols] + far(1, 1, cols) + near(0, 1, cols)


def merge(name, kernel, rows, tile, ins, outs, after=()):
    return pl.pallas_call(
        functools.partial(kernel, rows, tile),
        out_shape=outs,
        in_specs=[VMEM] * len(ins) + [pl.BlockSpec(memory_space=pl.ANY)] * len(after),
        out_specs=[VMEM] * len(outs),
        compiler_params=params(12),
        name=name,
    )(*ins, *after)


def last_kernel(rows, early, pick, own, arr0, arr1, *rest):
    tiles = own.shape[1] // SIDE // LANES
    readers = [Reader(a, own.shape[1] // 2, rows) for a in (arr0, arr1)]
    put = Writer(rest[-1])
    for t in range(tiles):
        at = (pick * tiles + t) * LANES
        added = jnp.concatenate([read(0, 1, slice(at, at + LANES)) for read in readers])
        tile = targets(early)[pick] * tiles + t
        put(own[:, pl.ds(pl.multiple_of(tile * LANES, LANES), LANES)] + added)
    put.close()


def last(name, rows, early, pick, own, arrivals, after=()):
    return pl.pallas_call(
        functools.partial(last_kernel, rows, early, pick),
        out_shape=[message(2 * rows, own.shape[1] // SIDE, True)],
        in_specs=[VMEM] * 3 + [pl.BlockSpec(memory_space=pl.ANY)] * len(after),
        out_specs=[VMEM],
        compiler_params=params(12),
        name=name,
    )(own, *arrivals, *after)


def cut_kernel(ref, *rest):
    out = rest[-1]
    wide = out.shape[1]
    at = pl.ds(pl.multiple_of((ref.shape[1] - wide) * (1 - coordinates()[3]), LANES), wide)
    out[...] = ref[:, at]


def own_columns(half, wide, core):
    start = (wide - half) * core
    for t in range(wide // LANES):
        lane = lax.broadcasted_iota(jnp.int32, (1, LANES), 1) + t * LANES
        yield slice(t * LANES, (t + 1) * LANES), (lane >= start) & (lane < start + half)


def held_kernel(rows, half, own0, own1, own2, own3, held_ref):
    core = coordinates()[3]
    wide = held_ref.shape[2]
    for k, ref in enumerate((own0, own1, own2, own3)):
        for cols, valid in own_columns(half, wide, core):
            at = pl.ds(pl.multiple_of((ref.shape[1] - wide) * core + cols.start, LANES), LANES)
            values = decode(ref[:rows, at], ref[rows : rows + 1, at].astype(F32))
            held_ref[k, :, cols] = jnp.where(valid, values, 0.0)


def gram_kernel(rows, half, held, carr, g_ref, gram_ref):
    _, y, _, core = coordinates()
    m1, m2 = masks(core)
    wide = g_ref.shape[2]
    for k, (mask, mask_other) in enumerate(((0, 0), (m1, m2), (m2, m1), (2, 2))):
        for cols, valid in own_columns(half, wide, core):
            g_ref[(y ^ mask) * 2 + core, :, cols] = held[k, :, cols]
            other = decode(carr[k, :rows, cols], carr[k, rows : rows + 1, cols].astype(F32))
            g_ref[(y ^ mask_other) * 2 + 1 - core, :, cols] = jnp.where(valid, other, 0.0)
    nodes = g_ref.shape[0]
    pairs = [(i, j) for i in range(nodes) for j in range(i, nodes)]

    def body(r, sums):
        blocks = [g_ref[n, pl.ds(r * 8, 8), :] for n in range(nodes)]
        out = []
        for total, (i, j) in zip(sums, pairs):
            product = blocks[i] * blocks[j]
            for t in range(wide // 128):
                total = total + product[:, t * 128 : (t + 1) * 128]
            out.append(total)
        return tuple(out)

    sums = lax.fori_loop(0, rows // 8, body, tuple(jnp.zeros((8, 128), F32) for _ in pairs))
    filled = [jnp.sum(total, axis=0, keepdims=True) for total in sums]
    filled += [jnp.zeros((1, 128), F32)] * (-len(pairs) % 8)
    stacked = jnp.sum(jnp.concatenate(filled), axis=1, keepdims=True)
    shape = (len(filled), 128)
    on = lax.broadcasted_iota(jnp.int32, shape, 0) == lax.broadcasted_iota(jnp.int32, shape, 1)
    row = jnp.sum(jnp.where(on, jnp.broadcast_to(stacked, shape), 0.0), axis=0, keepdims=True)
    gram_ref[...] = jnp.broadcast_to(row, gram_ref.shape)


def combine_kernel(half, g_ref, sums_ref, out_ref):
    nodes, rows, wide = g_ref.shape
    sums = jnp.sum(sums_ref[...], axis=0, keepdims=True)
    pairs = [(i, j) for i in range(nodes) for j in range(i, nodes)]
    gram = {}
    for k, (i, j) in enumerate(pairs):
        gram[i, j] = gram[j, i] = sums[:, k : k + 1]

    def inner(u, v):
        total = None
        for i, a in u.items():
            row = None
            for j, b in v.items():
                term = gram[i, j] * b
                row = term if row is None else row + term
            total = a * row if total is None else total + a * row
        return total

    one = jnp.ones((1, 1), F32)
    vectors = [{n: one} for n in range(nodes)]
    while len(vectors) > 1:
        middle = len(vectors) // 2
        merged = []
        for u, v in zip(vectors[:middle], vectors[middle:]):
            dot = inner(u, v)
            cu = 1.0 - dot / (2.0 * (inner(u, u) + EPS))
            cv = 1.0 - dot / (2.0 * (inner(v, v) + EPS))
            merged.append({**{n: cu * a for n, a in u.items()}, **{n: cv * a for n, a in v.items()}})
        vectors = merged
    total = None
    for n, coefficient in vectors[0].items():
        term = coefficient * g_ref[n]
        total = term if total is None else total + term
    core = lax.rem(lax.axis_index("node"), 2)
    moved = pltpu.roll(total, half, 1)
    out_ref[...] = jnp.where(core == 0, total[:, :half], moved[:, :half])


def local(x, dy):
    cols = dy.shape[1]
    rows = x.shape[1] // (2 * SIDE * SIDE)
    half = cols // (2 * SIDE)
    wide = -(-half // 128) * 128
    axes = ("x", "z")
    core = coordinates()[3]

    def send(pair, primary, is_first):
        return [exchange(m, axes[s] if primary else axes[1 - s], is_first) for s, m in enumerate(pair)]

    make = functools.partial(product, rows=rows, tile=256)
    xt, dyv, *m1 = first(rows, 256, x, dy)
    p1a_near = send(m1, True, True)
    m2 = make("p1a_far", xt=xt, dy=dyv, arrivals=[], after=m1)
    p1a_far = send(m2, True, True)
    p1b_near = send(make("p1b_near", xt=xt, dy=dyv, arrivals=[], after=m2), True, True)
    whole = ((0, 0, 2),)
    p2_near = send(make("p2_near", xt=xt, dy=dyv, arrivals=p1a_near, after=p1a_near, pieces=whole), True, False)
    m5 = make("p1b_far", xt=xt, dy=dyv, arrivals=[], after=p1a_far)
    p1b_far = send(m5, True, True)
    p2_far = send(make("p2_far", xt=xt, dy=dyv, arrivals=p1a_far, after=m5, pieces=whole), True, False)
    kept_near = make("kept_near", xt=xt, dy=dyv, arrivals=p1b_near, after=p1b_near, pieces=whole, coded=False)
    kept_far = make("kept_far", xt=xt, dy=dyv, arrivals=p1b_far, after=p1b_far, pieces=whole, coded=False)
    one = [message(rows, cols, False)] * 2
    q1_near = send(merge("q1_near", near_kernel, rows, 256, [*kept_near, *p2_near], one), False, True)
    q1_far = send(merge("q1_far", far_kernel, rows, 256, [*kept_near, *p2_near], one, p1b_far), False, True)
    half_of = [message(rows, cols // 2)] * 2
    m9 = merge("q2_early", q2_kernel, rows, True, [*kept_far, *p2_far, *q1_near], half_of)
    q2_early = send(m9, False, False)
    q2_late = send(merge("q2_late", q2_kernel, rows, False, [*kept_far, *p2_far, *q1_near], half_of, m9), False, False)
    own = merge("own", own_kernel, rows, 256, [*kept_far, *p2_far, *q1_far], [jax.ShapeDtypeStruct((2 * rows, cols), F32)])[0]
    far = last("last_far", rows, True, 0, own, q2_early)
    near1 = last("last_near1", rows, True, 1, own, q2_early, far)
    near2 = last("last_near2", rows, False, 0, own, q2_late, near1)
    mine = last("last_mine", rows, False, 1, own, q2_late, near2)[0]
    far, near1, near2 = far[0], near1[0], near2[0]
    far = lax.ppermute(far, "node", [(i, i ^ 4) for i in range(2 * SIDE)])
    near1 = exchange(near1, "y", True)
    near2 = exchange(near2, "y", False)
    blocks = [mine, near1, near2, far]
    cuts, before = [], []
    for name, k in (("far", 3), ("near1", 1), ("near2", 2), ("mine", 0)):
        cut = pl.pallas_call(
            cut_kernel,
            out_shape=jax.ShapeDtypeStruct((blocks[0].shape[0], wide), BF16),
            in_specs=[VMEM] + [pl.BlockSpec(memory_space=pl.ANY)] * len(before),
            out_specs=VMEM,
            compiler_params=params(12),
            name="cut_" + name,
        )(blocks[k], *before)
        before = [cut] if name != "near2" else before
        cuts.append(cut)
    far_cut, near1_cut, near2_cut, mine_cut = cuts
    across = jnp.stack([mine_cut, near1_cut, near2_cut, far_cut])
    carr = lax.ppermute(across, "node", [(i, i ^ 1) for i in range(2 * SIDE)])
    count = 2 * SIDE * SIDE * SIDE
    held = pl.pallas_call(
        functools.partial(held_kernel, 2 * rows, half),
        out_shape=jax.ShapeDtypeStruct((SIDE, 2 * rows, wide), F32),
        in_specs=[VMEM] * SIDE,
        out_specs=VMEM,
        compiler_params=params(12),
        name="held",
    )(*blocks)
    g, gram = pl.pallas_call(
        functools.partial(gram_kernel, 2 * rows, half),
        out_shape=[
            jax.ShapeDtypeStruct((2 * SIDE, 2 * rows, wide), F32),
            jax.ShapeDtypeStruct((count, 128), F32),
        ],
        compiler_params=params(12),
        name="gram",
    )(held, carr)
    sums = lax.all_to_all(gram, ("node", "fsdp"), 0, 0, tiled=True)
    return pl.pallas_call(
        functools.partial(combine_kernel, half),
        out_shape=jax.ShapeDtypeStruct((2 * rows, half), F32),
        compiler_params=params(12),
        name="combine",
    )(g, sums)


def solution(mesh):
    in_specs = (P(("node", "fsdp"), None), P(("node", "fsdp"), None))
    out_specs = P("fsdp", "node")
    return jax.shard_map(local, mesh=mesh, in_specs=in_specs, out_specs=out_specs, check_vma=False)
```

```python
import functools

import jax
import jax.numpy as jnp
from jax import lax
from jax.experimental import pallas as pl
from jax.experimental.pallas import tpu as pltpu
from jax.sharding import PartitionSpec as P

EPS = 1e-06
POWER = 17
TOP = 2.0 ** (124 / POWER)
TINY = 2.0**-118
LANES = 128
WIDE_ROWS = 8
GROUP = 16
SIDE = 4
BF16, F32 = jnp.bfloat16, jnp.float32


def encode(values):
    peak = jnp.maximum(jnp.max(jnp.abs(values), axis=0, keepdims=True), TINY).astype(BF16).astype(F32)
    x = values * (TOP / peak)
    x2 = x * x
    x4 = x2 * x2
    x8 = x4 * x4
    return (x8 * x8 * x).astype(BF16), peak


def decode(code, peak):
    code = code.astype(F32)
    size = jnp.exp(jnp.log(jnp.abs(code)) * (1.0 / POWER))
    return jnp.where(code < 0, -size, size) * (peak * (1.0 / TOP))


def scale_rows(tiles):
    return -(-tiles // GROUP) * GROUP


def message(rows, cols, wide=False):
    tiles = cols // LANES
    if wide:
        return jax.ShapeDtypeStruct((rows + WIDE_ROWS, cols), BF16)
    return jax.ShapeDtypeStruct((tiles * rows + scale_rows(tiles), LANES), BF16)


class Reader:
    def __init__(self, ref, cols, rows):
        self.ref, self.rows = ref, rows
        tiles = cols // LANES
        self.wide = ref.shape[1] == cols
        if self.wide:
            self.height = ref.shape[0] - WIDE_ROWS
            return
        self.height = (ref.shape[0] - scale_rows(tiles)) // tiles
        self.scales = ref[tiles * self.height :, :].astype(F32)

    def __call__(self, at, count, cols):
        if self.wide:
            values = self.ref[at * self.rows : (at + count) * self.rows, cols]
            return decode(values, self.ref[self.height : self.height + 1, cols].astype(F32))
        out = []
        for t in range(cols.start // LANES, cols.stop // LANES):
            first = t * self.height + at * self.rows
            out.append(decode(self.ref[first : first + count * self.rows, :], self.scales[t : t + 1]))
        return jnp.concatenate(out, axis=1)

    def dynamic(self, tile):
        if self.wide:
            cols = pl.ds(pl.multiple_of(tile * LANES, LANES), LANES)
            return decode(self.ref[: self.height, cols], self.ref[self.height : self.height + 1, cols].astype(F32))
        on = lax.broadcasted_iota(jnp.int32, self.scales.shape, 0) == tile
        peak = jnp.sum(jnp.where(on, self.scales, 0.0), axis=0, keepdims=True)
        first = pl.multiple_of(tile * self.height, GROUP)
        return decode(self.ref[pl.ds(first, self.height), :], peak)


class Writer:
    def __init__(self, out):
        self.out, self.at, self.peaks = out, 0, []

    def __call__(self, values):
        code, peak = encode(values)
        rows, width = values.shape
        if self.out.shape[1] > LANES:
            cols = slice(self.at, self.at + width)
            self.out[:rows, cols] = code
            self.out[rows:, cols] = jnp.broadcast_to(peak, (WIDE_ROWS, width)).astype(BF16)
            self.at += width
            return
        for t in range(0, values.shape[1], LANES):
            self.out[self.at : self.at + rows, :] = code[:, t : t + LANES]
            self.at += rows
            self.peaks.append(peak[:, t : t + LANES])

    def close(self):
        if self.out.shape[1] > LANES:
            return
        spare = [jnp.zeros((1, LANES), F32)] * (scale_rows(len(self.peaks)) - len(self.peaks))
        self.out[self.at :, :] = jnp.concatenate(self.peaks + spare).astype(BF16)


def coordinates():
    node, fsdp = lax.axis_index("node"), lax.axis_index("fsdp")
    return lax.rem(fsdp, SIDE), node // 2, fsdp // SIDE, lax.rem(node, 2)


def masks(core):
    return 1 + 2 * core, 3 - 2 * core


def pairing(axis, first):
    pairs = []
    for y in range(SIDE):
        for core in range(2):
            mask = masks(core)[0 if first else 1]
            for z in range(SIDE):
                for x in range(SIDE):
                    at = dict(x=x, y=y, z=z)
                    to = dict(at)
                    to[axis] ^= mask
                    index = lambda p: (p["y"] * 2 + core) * SIDE * SIDE + p["z"] * SIDE + p["x"]
                    pairs.append((index(at), index(to)))
    return pairs


def exchange(array, axis, first):
    return lax.ppermute(array, ("node", "fsdp"), pairing(axis, first))


def block_offset(stream, p, q, rows):
    owner = jnp.where(stream == 0, q * SIDE + p, p * SIDE + q)
    return pl.multiple_of((owner * 2 + stream) * rows, 16)


def wanted(which, rows):
    x, _, z, core = coordinates()
    m1, m2 = masks(core)
    offsets = []
    for stream in range(2):
        p, q = (x, z) if stream == 0 else (z, x)
        everything = [q ^ 2, q ^ m1, q ^ m2, q]
        ps, qs = {
            "p1a_near": (p ^ 2, everything[:2]),
            "p1a_far": (p ^ 2, everything[2:]),
            "p1b_near": (p ^ m1, everything[:2]),
            "p1b_far": (p ^ m1, everything[2:]),
            "p2_near": (p ^ m2, everything[:2]),
            "p2_far": (p ^ m2, everything[2:]),
            "kept_near": (p, everything[:2]),
            "kept_far": (p, everything[2:]),
        }[which]
        offsets.append([block_offset(stream, ps, each, rows) for each in qs])
    return offsets


def gather(xt_ref, lhs, offsets, rows):
    for s in range(2):
        for b, offset in enumerate(offsets[s]):
            at = (s * len(offsets[s]) + b) * rows
            lhs[at : at + rows, :] = xt_ref[pl.ds(offset, rows), :]


def first_kernel(rows, tile, x_ref, dy_ref, xt_ref, dy_vmem, out0, out1, x_vmem, lhs, x_sems, dy_sems):
    x_rows = [pl.ds(at, tile) for at in range(0, x_ref.shape[0], tile)]
    dy_cols = [pl.ds(at, 2 * tile) for at in range(0, dy_ref.shape[1], 2 * tile)]
    x_copies = [pltpu.make_async_copy(x_ref.at[r, :], x_vmem.at[r, :], x_sems.at[t]) for t, r in enumerate(x_rows)]
    dy_copies = [pltpu.make_async_copy(dy_ref.at[:, c], dy_vmem.at[:, c], dy_sems.at[t]) for t, c in enumerate(dy_cols)]
    for copy in x_copies:
        copy.start()
    for t, (at, copy) in enumerate(zip(range(0, x_ref.shape[0], tile), x_copies)):
        copy.wait()
        if t == len(x_copies) // 2 - 1:
            dy_copies[0].start()
        if t == len(x_copies) - 1:
            for other in dy_copies[1:]:
                other.start()
        for cols in parts_of(x_ref, tile):
            xt_ref[cols, at : at + tile] = x_vmem[at : at + tile, cols].T
    gather(xt_ref, lhs, wanted("p1a_near", rows), rows)
    size = 2 * rows
    writers = [Writer(out0), Writer(out1)]
    for t, copy in enumerate(dy_copies):
        copy.wait()
        for cols in (slice(2 * t * tile, (2 * t + 1) * tile), slice((2 * t + 1) * tile, (2 * t + 2) * tile)):
            total = jnp.dot(lhs[...], dy_vmem[:, cols], preferred_element_type=F32)
            for s, put in enumerate(writers):
                put(total[s * size : (s + 1) * size])
    for put in writers:
        put.close()


def product_kernel(which, rows, tile, coded, pieces, xt_ref, dy_ref, *rest):
    arrivals, (_, _, out0, out1, lhs) = rest[:-5], rest[-5:]
    offsets = wanted(which, rows)
    size = len(offsets[0]) * rows
    gather(xt_ref, lhs, offsets, rows)
    readers = [Reader(ref, dy_ref.shape[1], rows) for ref in arrivals]
    writers = [Writer(out0), Writer(out1)]
    for cols in parts_of(dy_ref, tile):
        total = jnp.dot(lhs[...], dy_ref[:, cols], preferred_element_type=F32)
        for s, out in enumerate((out0, out1)):
            part = total[s * size : (s + 1) * size]
            if pieces:
                part += jnp.concatenate([readers[2 * k + s](at, count, cols) for k, at, count in pieces])
            if coded:
                writers[s](part)
            else:
                out[:, cols] = part
    if coded:
        for put in writers:
            put.close()


def params(mib):
    return pltpu.CompilerParams(vmem_limit_bytes=mib * 2**20)


def column(i):
    return (0, i)


VMEM = pl.BlockSpec(memory_space=pltpu.VMEM)


def product(which, rows, tile, xt, dy, arrivals, after, count=2, pieces=(), coded=True):
    tokens, cols = dy.shape
    size = count * rows
    shape = message(size, cols, False) if coded else jax.ShapeDtypeStruct((size, cols), F32)
    return pl.pallas_call(
        functools.partial(product_kernel, which, rows, tile, coded, pieces),
        out_shape=[shape, shape],
        in_specs=[VMEM] * (2 + len(arrivals)) + [pl.BlockSpec(memory_space=pl.ANY)] * 2,
        out_specs=[VMEM] * 2,
        scratch_shapes=[pltpu.VMEM((2 * size, tokens), BF16)],
        compiler_params=params(12),
        name=which,
    )(xt, dy, *arrivals, *after)


def first(rows, tile, x, dy):
    tokens, cols = dy.shape
    xt = jax.ShapeDtypeStruct((x.shape[1], tokens), BF16)
    return pl.pallas_call(
        functools.partial(first_kernel, rows, tile),
        out_shape=[xt, jax.ShapeDtypeStruct(dy.shape, BF16)] + [message(2 * rows, cols, False)] * 2,
        in_specs=[pl.BlockSpec(memory_space=pltpu.HBM)] * 2,
        out_specs=[VMEM] * 4,
        scratch_shapes=[
            pltpu.VMEM(x.shape, BF16),
            pltpu.VMEM((4 * rows, tokens), BF16),
            pltpu.SemaphoreType.DMA((tokens // tile,)),
            pltpu.SemaphoreType.DMA((cols // (2 * tile),)),
        ],
        compiler_params=params(40),
        name="p1a_near",
    )(x, dy)


def parts_of(ref, tile):
    for at in range(0, ref.shape[1], tile):
        yield slice(at, at + tile)


def near_kernel(rows, tile, kept0, kept1, arr0, arr1, *rest):
    for kept, arr, out in ((kept0, arr0, rest[-2]), (kept1, arr1, rest[-1])):
        read, put = Reader(arr, kept.shape[1], rows), Writer(out)
        for cols in parts_of(kept, tile):
            put(kept[:rows, cols] + read(0, 1, cols))
        put.close()


def far_kernel(rows, tile, kept0, kept1, arr0, arr1, *rest):
    for kept, arr, out in ((kept0, arr0, rest[-2]), (kept1, arr1, rest[-1])):
        read, put = Reader(arr, kept.shape[1], rows), Writer(out)
        for cols in parts_of(kept, tile):
            put(kept[rows:, cols] + read(1, 1, cols))
        put.close()


def targets(early):
    _, y, _, core = coordinates()
    m1, m2 = masks(core)
    return (y ^ 2, y ^ m1) if early else (y ^ m2, y)


def q2_kernel(rows, early, kept0, kept1, p0, p1, q0, q1, *rest):
    cols = kept0.shape[1]
    tiles = cols // SIDE // LANES
    for kept, p, q, out in ((kept0, p0, q0, rest[-2]), (kept1, p1, q1, rest[-1])):
        far, near, put = Reader(p, cols, rows), Reader(q, cols, rows), Writer(out)
        for target in targets(early):
            for t in range(tiles):
                tile = target * tiles + t
                at = pl.ds(pl.multiple_of(tile * LANES, LANES), LANES)
                put(kept[:rows, at] + far.dynamic(tile)[:rows] + near.dynamic(tile))
        put.close()


def own_kernel(rows, tile, kept0, kept1, p0, p1, q0, q1, out):
    for s, (kept, p, q) in enumerate(((kept0, p0, q0), (kept1, p1, q1))):
        far, near = Reader(p, kept.shape[1], rows), Reader(q, kept.shape[1], rows)
        for cols in parts_of(kept, tile):
            out[s * rows : (s + 1) * rows, cols] = kept[rows:, cols] + far(1, 1, cols) + near(0, 1, cols)


def merge(name, kernel, rows, tile, ins, outs, after=()):
    return pl.pallas_call(
        functools.partial(kernel, rows, tile),
        out_shape=outs,
        in_specs=[VMEM] * len(ins) + [pl.BlockSpec(memory_space=pl.ANY)] * len(after),
        out_specs=[VMEM] * len(outs),
        compiler_params=params(12),
        name=name,
    )(*ins, *after)


def last_kernel(rows, early, pick, own, arr0, arr1, *rest):
    tiles = own.shape[1] // SIDE // LANES
    readers = [Reader(a, own.shape[1] // 2, rows) for a in (arr0, arr1)]
    put = Writer(rest[-1])
    for t in range(tiles):
        at = (pick * tiles + t) * LANES
        added = jnp.concatenate([read(0, 1, slice(at, at + LANES)) for read in readers])
        tile = targets(early)[pick] * tiles + t
        put(own[:, pl.ds(pl.multiple_of(tile * LANES, LANES), LANES)] + added)
    put.close()


def last(name, rows, early, pick, own, arrivals, after=()):
    return pl.pallas_call(
        functools.partial(last_kernel, rows, early, pick),
        out_shape=[message(2 * rows, own.shape[1] // SIDE, True)],
        in_specs=[VMEM] * 3 + [pl.BlockSpec(memory_space=pl.ANY)] * len(after),
        out_specs=[VMEM],
        compiler_params=params(12),
        name=name,
    )(own, *arrivals, *after)


def cut_kernel(ref, *rest):
    cuts, out = rest[:-1], rest[-1]
    wide = out.shape[-1]
    at = pl.ds(pl.multiple_of((ref.shape[1] - wide) * (1 - coordinates()[3]), LANES), wide)
    if len(cuts) < 3:
        out[...] = ref[:, at]
        return
    out[2] = ref[:, at]
    for k, held in zip((0, 1, 3), cuts):
        out[k] = held[...]


def own_columns(half, wide, core):
    start = (wide - half) * core
    for t in range(wide // LANES):
        lane = lax.broadcasted_iota(jnp.int32, (1, LANES), 1) + t * LANES
        yield slice(t * LANES, (t + 1) * LANES), (lane >= start) & (lane < start + half)


def held_kernel(rows, half, own0, own1, own2, own3, held_ref):
    core = coordinates()[3]
    wide = held_ref.shape[2]
    for k, ref in enumerate((own0, own1, own2, own3)):
        for cols, valid in own_columns(half, wide, core):
            at = pl.ds(pl.multiple_of((ref.shape[1] - wide) * core + cols.start, LANES), LANES)
            values = decode(ref[:rows, at], ref[rows : rows + 1, at].astype(F32))
            held_ref[k, :, cols] = jnp.where(valid, values, 0.0)


def gram_kernel(rows, half, held, carr, g_ref, gram_ref):
    _, y, _, core = coordinates()
    m1, m2 = masks(core)
    wide = g_ref.shape[2]
    for k, (mask, mask_other) in enumerate(((0, 0), (m1, m2), (m2, m1), (2, 2))):
        for cols, valid in own_columns(half, wide, core):
            g_ref[(y ^ mask) * 2 + core, :, cols] = held[k, :, cols]
            other = decode(carr[k, :rows, cols], carr[k, rows : rows + 1, cols].astype(F32))
            g_ref[(y ^ mask_other) * 2 + 1 - core, :, cols] = jnp.where(valid, other, 0.0)
    nodes = g_ref.shape[0]
    pairs = [(i, j) for i in range(nodes) for j in range(i, nodes)]

    def body(r, sums):
        blocks = [g_ref[n, pl.ds(r * 8, 8), :] for n in range(nodes)]
        out = []
        for total, (i, j) in zip(sums, pairs):
            product = blocks[i] * blocks[j]
            for t in range(wide // 128):
                total = total + product[:, t * 128 : (t + 1) * 128]
            out.append(total)
        return tuple(out)

    sums = lax.fori_loop(0, rows // 8, body, tuple(jnp.zeros((8, 128), F32) for _ in pairs))
    filled = [jnp.sum(total, axis=0, keepdims=True) for total in sums]
    filled += [jnp.zeros((1, 128), F32)] * (-len(pairs) % 8)
    stacked = jnp.sum(jnp.concatenate(filled), axis=1, keepdims=True)
    shape = (len(filled), 128)
    on = lax.broadcasted_iota(jnp.int32, shape, 0) == lax.broadcasted_iota(jnp.int32, shape, 1)
    row = jnp.sum(jnp.where(on, jnp.broadcast_to(stacked, shape), 0.0), axis=0, keepdims=True)
    gram_ref[...] = jnp.broadcast_to(row, gram_ref.shape)


def combine_kernel(half, g_ref, sums_ref, out_ref):
    nodes, rows, wide = g_ref.shape
    sums = jnp.sum(sums_ref[...], axis=0, keepdims=True)
    pairs = [(i, j) for i in range(nodes) for j in range(i, nodes)]
    gram = {}
    for k, (i, j) in enumerate(pairs):
        gram[i, j] = gram[j, i] = sums[:, k : k + 1]

    def inner(u, v):
        total = None
        for i, a in u.items():
            row = None
            for j, b in v.items():
                term = gram[i, j] * b
                row = term if row is None else row + term
            total = a * row if total is None else total + a * row
        return total

    one = jnp.ones((1, 1), F32)
    vectors = [{n: one} for n in range(nodes)]
    while len(vectors) > 1:
        middle = len(vectors) // 2
        merged = []
        for u, v in zip(vectors[:middle], vectors[middle:]):
            dot = inner(u, v)
            cu = 1.0 - dot / (2.0 * (inner(u, u) + EPS))
            cv = 1.0 - dot / (2.0 * (inner(v, v) + EPS))
            merged.append({**{n: cu * a for n, a in u.items()}, **{n: cv * a for n, a in v.items()}})
        vectors = merged
    total = None
    for n, coefficient in vectors[0].items():
        term = coefficient * g_ref[n]
        total = term if total is None else total + term
    core = lax.rem(lax.axis_index("node"), 2)
    moved = pltpu.roll(total, half, 1)
    out_ref[...] = jnp.where(core == 0, total[:, :half], moved[:, :half])


def local(x, dy):
    cols = dy.shape[1]
    rows = x.shape[1] // (2 * SIDE * SIDE)
    half = cols // (2 * SIDE)
    wide = -(-half // 128) * 128
    axes = ("x", "z")
    core = coordinates()[3]

    def send(pair, primary, is_first):
        return [exchange(m, axes[s] if primary else axes[1 - s], is_first) for s, m in enumerate(pair)]

    make = functools.partial(product, rows=rows, tile=256)
    xt, dyv, *m1 = first(rows, 256, x, dy)
    p1a_near = send(m1, True, True)
    m2 = make("p1a_far", xt=xt, dy=dyv, arrivals=[], after=m1)
    p1a_far = send(m2, True, True)
    p1b_near = send(make("p1b_near", xt=xt, dy=dyv, arrivals=[], after=m2), True, True)
    whole = ((0, 0, 2),)
    p2_near = send(make("p2_near", xt=xt, dy=dyv, arrivals=p1a_near, after=p1a_near, pieces=whole), True, False)
    m5 = make("p1b_far", xt=xt, dy=dyv, arrivals=[], after=p1a_far)
    p1b_far = send(m5, True, True)
    p2_far = send(make("p2_far", xt=xt, dy=dyv, arrivals=p1a_far, after=m5, pieces=whole), True, False)
    kept_near = make("kept_near", xt=xt, dy=dyv, arrivals=p1b_near, after=p1b_near, pieces=whole, coded=False)
    kept_far = make("kept_far", xt=xt, dy=dyv, arrivals=p1b_far, after=p1b_far, pieces=whole, coded=False)
    one = [message(rows, cols, False)] * 2
    q1_near = send(merge("q1_near", near_kernel, rows, 256, [*kept_near, *p2_near], one), False, True)
    q1_far = send(merge("q1_far", far_kernel, rows, 256, [*kept_near, *p2_near], one, p1b_far), False, True)
    half_of = [message(rows, cols // 2)] * 2
    m9 = merge("q2_early", q2_kernel, rows, True, [*kept_far, *p2_far, *q1_near], half_of)
    q2_early = send(m9, False, False)
    q2_late = send(merge("q2_late", q2_kernel, rows, False, [*kept_far, *p2_far, *q1_near], half_of, m9), False, False)
    own = merge("own", own_kernel, rows, 256, [*kept_far, *p2_far, *q1_far], [jax.ShapeDtypeStruct((2 * rows, cols), F32)])[0]
    far = last("last_far", rows, True, 0, own, q2_early)
    near1 = last("last_near1", rows, True, 1, own, q2_early, far)
    near2 = last("last_near2", rows, False, 0, own, q2_late, near1)
    mine = last("last_mine", rows, False, 1, own, q2_late, near2)[0]
    far, near1, near2 = far[0], near1[0], near2[0]
    far = lax.ppermute(far, "node", [(i, i ^ 4) for i in range(2 * SIDE)])
    near1 = exchange(near1, "y", True)
    near2 = exchange(near2, "y", False)
    blocks = [mine, near1, near2, far]
    def cut(name, block, before):
        shape = (block.shape[0], wide)
        return pl.pallas_call(
            cut_kernel,
            out_shape=jax.ShapeDtypeStruct(shape if len(before) < 3 else (SIDE, *shape), BF16),
            in_specs=[VMEM] * (1 + len(before)),
            out_specs=VMEM,
            compiler_params=params(12),
            name="cut_" + name,
        )(block, *before)

    far_cut = cut("far", far, [])
    near1_cut = cut("near1", near1, [far_cut])
    across = cut("near2", near2, [cut("mine", mine, []), near1_cut, far_cut])
    carr = lax.ppermute(across, "node", [(i, i ^ 1) for i in range(2 * SIDE)])
    count = 2 * SIDE * SIDE * SIDE
    held = pl.pallas_call(
        functools.partial(held_kernel, 2 * rows, half),
        out_shape=jax.ShapeDtypeStruct((SIDE, 2 * rows, wide), F32),
        in_specs=[VMEM] * SIDE,
        out_specs=VMEM,
        compiler_params=params(12),
        name="held",
    )(*blocks)
    g, gram = pl.pallas_call(
        functools.partial(gram_kernel, 2 * rows, half),
        out_shape=[
            jax.ShapeDtypeStruct((2 * SIDE, 2 * rows, wide), F32),
            jax.ShapeDtypeStruct((count, 128), F32),
        ],
        compiler_params=params(12),
        name="gram",
    )(held, carr)
    sums = lax.all_to_all(gram, ("node", "fsdp"), 0, 0, tiled=True)
    return pl.pallas_call(
        functools.partial(combine_kernel, half),
        out_shape=jax.ShapeDtypeStruct((2 * rows, half), F32),
        compiler_params=params(12),
        name="combine",
    )(g, sums)


def solution(mesh):
    in_specs = (P(("node", "fsdp"), None), P(("node", "fsdp"), None))
    out_specs = P("fsdp", "node")
    return jax.shard_map(local, mesh=mesh, in_specs=in_specs, out_specs=out_specs, check_vma=False)
```
